32 devices in a mesh: seg: 8 (over z, y), head: 4 (over x, core).
Axes of the slice: x: 2, y: 2, z: 4, core: 2. Of those that a mesh axis runs over, the one named last changes fastest.
Arguments:
- queries: bfloat16 [2048, 2048], P('seg', 'head'), may hold values from -20 to 20
- keys: bfloat16 [2048, 2048], P('seg', 'head'), may hold values from -12 to 12
- values: bfloat16 [2048, 2048], P('seg', 'head'), may hold values from -6 to 6
- out_grad: bfloat16 [2048, 2048], P('seg', 'head'), may hold values from -2.5 to 2.5
- out_weight: bfloat16 [2048, 2048], P('head'), may hold values from -1 to 1
- retr_owner: int32 [8, 4], replicated, may hold values from 0 to 7, as said below
- retr_block: int32 [8, 4], replicated, may hold values from -1 to 1, as said below
Outputs:
- layer_out: bfloat16 [2048, 2048], P('seg', 'head')
- query_grad: bfloat16 [2048, 2048], P('seg', 'head')
- key_grad: bfloat16 [2048, 2048], P('seg', 'head')
- value_grad: bfloat16 [2048, 2048], P('seg', 'head')
- proj_grad_t: float32 [2048, 2048], P('seg', 'head')
The draws below stay inside these ranges and needn't reach their ends.
Inputs may be any that keep to these rules, and one draw needn't show every extreme that they name: `retr_owner`: row s lists 4 owners, all different from one another and from s. `retr_block`: padding (-1) comes after the live entries of a row; every row has at least 3 live entries.
All inputs are finite; a program needn't handle non-finite values.
Results may differ from the reference program's by a relative error of at most 0.012.
Values may be sent and summed in bfloat16 or wider, within the bound.
No kernel may reach another device: no remote copies, remote signals or barrier semaphores. Data moves between devices by JAX's collectives and lax.ppermute only.
A program may use at most 128 MiB of HBM per device.

```python
import math
import jax
import jax.numpy as jnp
from jax import lax

D = 2048
HEADS = 16
DH = 128
BLOCK = 128
SEG = 256
SEGMENTS = 8
TOKENS = 2048
MEMB = 2
R = 4


def draw_queries(key, part):
    spread = 2.0 * jnp.clip(jax.random.normal(jax.random.fold_in(key, 1), (TOKENS, HEADS * DH), jnp.float32), -6.0, 6.0)
    return spread.astype(jnp.bfloat16)


def draw_keys(key, part):
    spread = jnp.clip(jax.random.normal(jax.random.fold_in(key, 2), (TOKENS, HEADS * DH), jnp.float32), -6.0, 6.0)
    return spread.astype(jnp.bfloat16)


def draw_retr_owner(key, part):
    streams = jax.random.split(jax.random.fold_in(key, 5), SEGMENTS)
    orders = jax.vmap(lambda stream: jax.random.permutation(stream, SEGMENTS - 1))(streams)[:, :R]
    return ((jnp.arange(SEGMENTS)[:, None] + 1 + orders) % SEGMENTS).astype(jnp.int32)


def draw_retr_block(key, part):
    first_key, second_key = jax.random.split(jax.random.fold_in(key, 7))
    blocks = jax.random.randint(first_key, (SEGMENTS, R), 0, MEMB)
    blocks = blocks.at[0, 0].set(MEMB - 1)
    live_count = jax.random.randint(second_key, (SEGMENTS,), R - R // 4, R + 1)
    live_count = live_count.at[0].set(R).at[1].set(R - R // 4)
    places = jnp.arange(R)
    return jnp.where(places[None, :] < live_count[:, None], blocks, -1).astype(jnp.int32)


def spiked(array, key, source, target, shards_of, factor):
    def block_of(dim):
        return (jnp.arange(array.shape[dim]) // (array.shape[dim] // shards_of)).reshape((-1,) + (1,) * (array.ndim - 1 - dim))

    first = jax.random.permutation(key, shards_of)[block_of(target)]
    far = (block_of(target) + shards_of // 2) % shards_of
    return jnp.where((block_of(source) == first) | (block_of(source) == far), factor * array, array)


def block_scale(key, shape, cuts, low, high):
    gain = 1.0
    for axis_at, parts in cuts:
        heights = jax.random.uniform(jax.random.fold_in(jax.random.fold_in(key, 6), axis_at), (parts,), jnp.float32, low / len(cuts), high / len(cuts))
        gain = gain * jnp.repeat(jnp.exp(heights), shape[axis_at] // parts).reshape((-1,) + (1,) * (len(shape) - 1 - axis_at))
    return gain


def scatter_about(rng, shape, deviation, bound, pieces=(), kind=jnp.bfloat16):
    entries = jax.random.normal(rng, shape, jnp.float32) * deviation
    if len(pieces) > 0:
        entries = block_scale(rng, shape, pieces, -0.22, 0.18) * entries
    return jnp.clip(entries, min=-bound, max=bound).astype(kind)


def gaussian_with(stream_key, extent, scale, bound, cuts, heavy, held_as=jnp.bfloat16):
    values = scale * jax.random.normal(stream_key, extent, jnp.float32)
    if cuts:
        values = values * block_scale(stream_key, extent, cuts, -0.22, 0.18)
    return jnp.clip(spiked(values, jax.random.fold_in(stream_key, 3), *heavy), -bound, bound).astype(held_as)


def setup_inputs(seed: int = 0) -> dict:
    splits = jax.random.split(jax.random.key(seed), 8)
    return {
        "queries": draw_queries(jax.random.fold_in(splits[7], 71), 0),
        "keys": draw_keys(jax.random.fold_in(splits[7], 71), 0),
        "values": scatter_about(splits[2], (TOKENS, HEADS * DH), 1.0, 6.0, ((0, 8), (1, 4))),
        "out_grad": gaussian_with(splits[3], (TOKENS, D), 0.125, 2.5, ((0, 8), (1, 4)), (0, 1, 8, 2.0)),
        "out_weight": scatter_about(splits[4], (HEADS * DH, D), (DH // 4) ** -0.5, 1.0, ((0, 4),)),
        "retr_owner": draw_retr_owner(jax.random.fold_in(splits[7], 71), 0),
        "retr_block": draw_retr_block(jax.random.fold_in(splits[7], 71), 0),
    }


def split_heads(tok_rows, count):
    return tok_rows.reshape(tok_rows.shape[0], count, -1).transpose(1, 0, 2)

def join_heads(stacked):
    return stacked.transpose(1, 0, 2).reshape(stacked.shape[1], -1)

def product(form, left_side, right_side):
    return jnp.einsum(form, left_side.astype(jnp.float32), right_side.astype(jnp.float32))

def attend(queries, keys, values, cache_k, cache_v, mem_k, mem_v, mem_live, has_cache, d_attn, score_scale):
    length = queries.shape[1]
    causal = jnp.arange(length)[:, None] >= jnp.arange(length)[None, :]
    own = jnp.where(causal[None], product('hqd,hkd->hqk', queries, keys) * score_scale, -jnp.inf)
    cached = jnp.where(has_cache, product('hqd,hkd->hqk', queries, cache_k) * score_scale, -jnp.inf)
    stored = jnp.where(mem_live[None, None, :], product('hqd,hkd->hqk', queries, mem_k) * score_scale, -jnp.inf)
    row_top = jnp.maximum(jnp.maximum(lax.optimization_barrier(jnp.max(own, -1)), lax.optimization_barrier(jnp.max(cached, -1))), lax.optimization_barrier(jnp.max(stored, -1)))[..., None]
    row_total = lax.optimization_barrier(jnp.sum(jnp.exp(own - row_top), -1)) + lax.optimization_barrier(jnp.sum(jnp.exp(cached - row_top), -1)) + lax.optimization_barrier(jnp.sum(jnp.exp(stored - row_top), -1))
    log_total = row_top + jnp.log(row_total)[..., None]
    weights = [jnp.exp(group_scores - log_total) for group_scores in (own, cached, stored)]
    rounded = [entry.astype(jnp.bfloat16) for entry in weights]
    sources = (values, cache_v, mem_v)
    mixed_sum = product('hqk,hkd->hqd', rounded[0], sources[0]) + product('hqk,hkd->hqd', rounded[1], sources[1]) + product('hqk,hkd->hqd', rounded[2], sources[2])
    attn = mixed_sum.astype(jnp.bfloat16)
    row_delta = lax.optimization_barrier(jnp.sum(d_attn.astype(jnp.float32) * attn.astype(jnp.float32), -1))[..., None]
    slopes = [(entry * (product('hqd,hkd->hqk', d_attn, source) - row_delta)).astype(jnp.bfloat16) for entry, source in zip(weights, sources)]
    grad_q = score_scale * (product('hqk,hkd->hqd', slopes[0], keys) + product('hqk,hkd->hqd', slopes[1], cache_k) + product('hqk,hkd->hqd', slopes[2], mem_k))
    grad_k_own = score_scale * product('hqk,hqd->hkd', slopes[0], queries)
    grad_v_own = product('hqk,hqd->hkd', rounded[0], d_attn)
    grad_k_cache = score_scale * product('hqk,hqd->hkd', slopes[1], queries)
    grad_v_cache = product('hqk,hqd->hkd', rounded[1], d_attn)
    return (attn, grad_q, grad_k_own, grad_v_own, grad_k_cache, grad_v_cache)

def reference(queries, keys, values, out_grad, out_weight, retr_owner, retr_block):
    score_scale = 1.0 / math.sqrt(DH)
    d_attn = jnp.dot(out_grad, out_weight.T, preferred_element_type=jnp.float32).astype(jnp.bfloat16)
    offsets = jnp.arange(BLOCK, dtype=jnp.int32)

    def one_segment(segment):

        def rows_at(source, begin):
            return split_heads(lax.dynamic_slice_in_dim(source, begin, SEG, 0), HEADS)
        start = (segment * SEG).astype(jnp.int32)
        previous = (jnp.maximum(segment - 1, 0) * SEG).astype(jnp.int32)
        owners = retr_owner[segment]
        blocks = retr_block[segment]
        picked = ((owners * SEG + jnp.maximum(blocks, 0) * BLOCK)[:, None] + offsets[None, :]).reshape(-1).astype(jnp.int32)
        mem_k = split_heads(keys[picked], HEADS)
        mem_v = split_heads(values[picked], HEADS)
        mem_live = jnp.repeat(blocks >= 0, BLOCK)
        results = attend(rows_at(queries, start), rows_at(keys, start), rows_at(values, start), rows_at(keys, previous), rows_at(values, previous), mem_k, mem_v, mem_live, segment > 0, rows_at(d_attn, start), score_scale)
        return tuple((join_heads(entry) for entry in results))
    attn, grad_q, grad_k_own, grad_v_own, grad_k_cache, grad_v_cache = lax.map(one_segment, jnp.arange(SEGMENTS, dtype=jnp.int32))
    carried_k = jnp.concatenate([grad_k_cache[1:], jnp.zeros_like(grad_k_cache[:1])], 0)
    carried_v = jnp.concatenate([grad_v_cache[1:], jnp.zeros_like(grad_v_cache[:1])], 0)
    attn_rows = attn.reshape(TOKENS, -1)
    layer_out = jnp.dot(attn_rows, out_weight, preferred_element_type=jnp.float32).astype(jnp.bfloat16)
    query_grad = grad_q.reshape(TOKENS, -1).astype(jnp.bfloat16)
    key_grad = (grad_k_own + carried_k).reshape(TOKENS, -1).astype(jnp.bfloat16)
    value_grad = (grad_v_own + carried_v).reshape(TOKENS, -1).astype(jnp.bfloat16)
    proj_grad_t = jnp.dot(out_grad.T, attn_rows, preferred_element_type=jnp.float32)
    return (layer_out, query_grad, key_grad, value_grad, proj_grad_t)
```

```python
import functools
import math

import jax
import jax.numpy as jnp
from jax import lax
from jax.experimental import pallas as pl
from jax.experimental.pallas import tpu as pltpu
from jax.sharding import PartitionSpec as P

DH = 128
BLOCK = 128
F32 = jnp.float32
BF16 = jnp.bfloat16
HIDDEN = -1e30
VMEM = pl.BlockSpec(memory_space=pltpu.VMEM)
SMEM = pl.BlockSpec(memory_space=pltpu.SMEM)


def dot(left, right, dims):
    return lax.dot_general(left, right, ((dims[:1], dims[1:]), ((), ())), preferred_element_type=F32)


def lanes(block, width):
    return pl.ds(pl.multiple_of(block * width, width), width)


def call(body, outs, operands, specs=None, scratch=(), flops=0):
    nbytes = sum(x.size * x.dtype.itemsize for x in (*operands, *outs))
    return pl.pallas_call(
        body,
        out_shape=outs,
        in_specs=specs or [VMEM] * len(operands),
        out_specs=[VMEM] * len(outs),
        scratch_shapes=list(scratch),
        compiler_params=pltpu.CompilerParams(vmem_limit_bytes=56 * 2**20),
        cost_estimate=pl.CostEstimate(flops=flops, bytes_accessed=nbytes, transcendentals=0),
    )(*operands)


def shape(dims, dtype):
    return jax.ShapeDtypeStruct(dims, dtype)


def cut_body(A, B, q_ref, k_ref, v_ref, *outs):
    a = lax.axis_index("seg") // B
    for m in range(A):
        head = lanes(a ^ m, DH)
        outs[m][:, :DH] = k_ref[:, head]
        outs[m][:, DH:] = v_ref[:, head]
        outs[A + m][...] = q_ref[:, head]


def slope_body(A, B, H, *refs):
    grads, weight_ref, outs = refs[:H], refs[H], refs[H + 1 : H + 1 + A]
    full, mixed = refs[H + 1 + A :]
    a = lax.axis_index("seg") // B
    h = lax.axis_index("head")
    width = grads[0].shape[1]
    for k in range(H):
        full[:, lanes(h ^ k, width)] = grads[k][...]
    mixed[...] = dot(full[...], weight_ref[...], (1, 1)).astype(BF16)
    for m in range(A):
        outs[m][:, :DH] = mixed[:, lanes(a ^ m, DH)]
        outs[m][:, DH:] = full[:, lanes((a ^ m) * H + h, width // H)]


def attend_body(A, B, R, score_scale, owner_ref, block_ref, *refs):
    pair = B == 2
    q_refs, dag_refs, refs = refs[:A], refs[A : 2 * A], refs[2 * A :]
    kv_refs, refs = (refs[: 2 * A], refs[2 * A :]) if pair else (refs[:1], refs[1:])
    attn_ref, dq_ref, own_ref, carry_ref, q_all, da_all, kv, kvcat = refs
    SEG = q_refs[0].shape[0]
    parts = SEG // BLOCK
    count = 2 * SEG + R * BLOCK
    seg = lax.axis_index("seg")
    a, b = seg // B, seg % B
    for m in range(A):
        q_all[m] = q_refs[m][...]
        da_all[m] = dag_refs[m][:, :DH]
    if pair:
        for i in range(2 * A):
            for part in range(parts):
                kv[i * parts + part] = kv_refs[i][part * BLOCK : (part + 1) * BLOCK, :]
    else:
        kv = kv_refs[0]

    def place(other_a, other_b):
        slot = (other_b ^ b) * A + (other_a ^ a) if pair else other_b * A + (other_a ^ a)
        return slot * parts

    def segment(m):
        seg_a = a ^ m
        s = seg_a * B + b
        prev_b = jnp.where(b == 0, B - 1, b - 1)
        prev_a = jnp.where(b == 0, (seg_a + A - 1) % A, seg_a)
        column = lax.broadcasted_iota(jnp.int32, (1, count), 1)
        hidden = (column >= SEG) & (column < 2 * SEG) & (s == 0)
        for part in range(parts):
            at = part * BLOCK
            kvcat[at : at + BLOCK] = kv[place(seg_a, b) + part]
            kvcat[SEG + at : SEG + at + BLOCK] = kv[place(prev_a, prev_b) + part]
        for j in range(R):
            at = 2 * SEG + j * BLOCK
            owner, block = owner_ref[s, j], block_ref[s, j]
            kvcat[at : at + BLOCK] = kv[place(owner // B, owner % B) + jnp.maximum(block, 0)]
            hidden |= (column >= at) & (column < at + BLOCK) & (block < 0)
        bias = jnp.where(hidden, HIDDEN, 0.0)
        q, da = q_all[m], da_all[m]
        keys, values = kvcat[:, :DH], kvcat[:, DH:]
        scores = dot(q, keys, (1, 1)) * score_scale + bias
        row = lax.broadcasted_iota(jnp.int32, (SEG, SEG), 0)
        col = lax.broadcasted_iota(jnp.int32, (SEG, SEG), 1)
        scores = jnp.concatenate([jnp.where(row >= col, scores[:, :SEG], HIDDEN), scores[:, SEG:]], 1)
        top = jnp.max(scores, -1, keepdims=True)
        grown = jnp.exp(scores - top)
        weights = grown * (1.0 / jnp.sum(grown, -1, keepdims=True))
        rounded = weights.astype(BF16)
        attn = dot(rounded, values, (1, 0)).astype(BF16)
        attn_ref[m] = attn
        row_delta = jnp.sum(da.astype(F32) * attn.astype(F32), -1, keepdims=True)
        slopes = (weights * (dot(da, values, (1, 1)) - row_delta)).astype(BF16)
        dq_ref[m] = (score_scale * dot(slopes, keys, (1, 0))).astype(BF16)
        dk = score_scale * dot(slopes[:, : 2 * SEG], q, (0, 0))
        dv = dot(rounded[:, : 2 * SEG], da, (0, 0))
        own_ref[m, :, :DH] = dk[:SEG]
        own_ref[m, :, DH:] = dv[:SEG]
        slot = prev_a ^ a
        carry_ref[slot, :, :DH] = dk[SEG:].astype(BF16)
        carry_ref[slot, :, DH:] = dv[SEG:].astype(BF16)

    if pair:
        for m in range(A):
            segment(m)
    else:
        lax.fori_loop(0, A, lambda m, _: segment(m), None)


def project_body(A, B, H, *refs):
    attns, gs, weight_ref, refs = refs[:A], refs[A : A + H], refs[A + H], refs[A + H + 1 :]
    keep_ref, send_ref, *proj_refs = refs[:-3]
    own, mixed, cots = refs[-3:]
    seg = lax.axis_index("seg")
    a, b = seg // B, seg % B
    h = lax.axis_index("head")
    SEG = attns[0].shape[1]
    for m in range(A):
        head = lanes(a ^ m, DH)
        own[:, head] = attns[m][m]
        for i in range(A):
            mixed[(m ^ i) * SEG : (m ^ i) * SEG + SEG, head] = attns[m][i]
    width = keep_ref.shape[1] // (H // 2)
    for k in range(0, H, 2):
        at = k // 2 * width
        keep_ref[:, at : at + width] = dot(own[...], weight_ref[:, lanes(h ^ k, width)], (1, 0))
        send_ref[:, at : at + width] = dot(own[...], weight_ref[:, lanes(h ^ (k + 1), width)], (1, 0)).astype(BF16)
    piece = gs[0].shape[2]
    for k in range(H):
        for m in range(A):
            cots[m * SEG : (m + 1) * SEG, lanes(h ^ k, piece)] = gs[k][m]
    if B == 2:
        rows = piece * H // 2
        proj_refs[0][...] = dot(cots[:, lanes(b, rows)], mixed[...], (0, 0))
        proj_refs[1][...] = dot(cots[:, lanes(1 - b, rows)], mixed[...], (0, 0)).astype(BF16)
    else:
        proj_refs[0][...] = dot(cots[...], mixed[...], (0, 0))


def merge_body(A, dq_ref, own_ref, carry_ref, *outs):
    for m in range(A):
        outs[m][:, :DH] = dq_ref[m]
        outs[m][:, DH:] = (own_ref[m] + carry_ref[m].astype(F32)).astype(BF16)


def place_body(A, B, *refs):
    pieces, outs = refs[:A], refs[A:]
    a = lax.axis_index("seg") // B
    for m in range(A):
        for i in range(3):
            outs[i][:, lanes(a ^ m, DH)] = pieces[m][:, i * DH : (i + 1) * DH]


def per_device(queries, keys, values, out_grad, out_weight, retr_owner, retr_block):
    n, H = lax.axis_size("seg"), lax.axis_size("head")
    SEG, width = queries.shape
    A = width // DH
    B = n // A
    R = retr_owner.shape[1]
    D = out_weight.shape[1]
    score_scale = 1.0 / math.sqrt(DH)

    def over_a(x, m):
        return lax.ppermute(x, "seg", [(i, (i // B ^ m) * B + i % B) for i in range(n)])

    def back_b(x):
        return lax.ppermute(x, "seg", [(i, i // B * B + (i % B - 1) % B) for i in range(n)])

    def over_head(x, k):
        return lax.ppermute(x, "head", [(i, i ^ k) for i in range(H)])

    def over_heads(x):
        parts = {0: x}
        for bit in (2, 1):
            parts |= {k | bit: over_head(parts[k], bit) for k in sorted(parts)}
        return [parts[k] for k in range(H)]

    grads = over_heads(out_grad)
    cut = call(
        functools.partial(cut_body, A, B),
        [shape((SEG, 2 * DH), BF16)] * A + [shape((SEG, DH), BF16)] * A,
        [queries, keys, values],
    )
    kvs = [cut[0]] + [over_a(cut[m], m) for m in range(1, A)]
    qs = [cut[A]] + [over_a(cut[A + m], m) for m in range(1, A)]
    if B == 2:
        kvs = kvs + [back_b(piece) for piece in kvs]
    else:
        groups = [[i * B + j for j in range(B)] for i in range(A)]
        gathered = lax.all_gather(jnp.stack(kvs), "seg", axis_index_groups=groups)
        kvs = [gathered.reshape(B * A * (SEG // BLOCK), BLOCK, 2 * DH)]
    dag = call(
        functools.partial(slope_body, A, B, H),
        [shape((SEG, 2 * DH), BF16)] * A,
        [*grads, out_weight],
        scratch=[pltpu.VMEM((SEG, D), BF16), pltpu.VMEM((SEG, width), BF16)],
        flops=2 * SEG * D * width,
    )
    dags = [dag[0]] + [over_a(dag[m], m) for m in range(1, A)]
    count = 2 * SEG + R * BLOCK
    attn, dq, own, carry = call(
        functools.partial(attend_body, A, B, R, score_scale),
        [
            shape((A, SEG, DH), BF16),
            shape((A, SEG, DH), BF16),
            shape((A, SEG, 2 * DH), F32),
            shape((A, SEG, 2 * DH), BF16),
        ],
        [retr_owner, retr_block, *qs, *dags, *kvs],
        specs=[SMEM] * 2 + [VMEM] * (2 * A + len(kvs)),
        scratch=[
            pltpu.VMEM((A, SEG, DH), BF16),
            pltpu.VMEM((A, SEG, DH), BF16),
            pltpu.VMEM((2 * A * (SEG // BLOCK), BLOCK, 2 * DH), BF16),
            pltpu.VMEM((count, 2 * DH), BF16),
        ],
        flops=10 * A * SEG * count * DH,
    )
    attns = [attn] + [over_a(attn, m) for m in range(1, A)]
    carried = back_b(carry)
    gs = over_heads(jnp.stack([piece[:, DH:] for piece in dags]))
    partials = [shape((SEG, D // 2), F32), shape((SEG, D // 2), BF16)]
    rows = D // A
    if B == 2:
        projs = [shape((rows // 2, width), F32), shape((rows // 2, width), BF16)]
    else:
        projs = [shape((rows, width), F32)]
    keep, send, *proj = call(
        functools.partial(project_body, A, B, H),
        partials + projs,
        [*attns, *gs, out_weight],
        scratch=[
            pltpu.VMEM((SEG, width), BF16),
            pltpu.VMEM((A * SEG, width), BF16),
            pltpu.VMEM((A * SEG, rows), BF16),
        ],
        flops=2 * SEG * width * D + 2 * A * SEG * rows * width,
    )
    block = D // H
    summed = keep + over_head(send, 1).astype(F32)
    layer_out = (summed[:, :block] + over_head(summed[:, block:].astype(BF16), 2).astype(F32)).astype(BF16)
    if B == 2:
        proj_grad_t = proj[0] + back_b(proj[1]).astype(F32)
    else:
        proj_grad_t = lax.psum_scatter(proj[0], "seg", scatter_dimension=0, axis_index_groups=groups, tiled=True)
    merged = call(
        functools.partial(merge_body, A), [shape((SEG, 3 * DH), BF16)] * A, [dq, own, carried]
    )
    placed = call(
        functools.partial(place_body, A, B),
        [shape((SEG, width), BF16)] * 3,
        [merged[0]] + [over_a(merged[m], m) for m in range(1, A)],
    )
    return (layer_out, *placed, proj_grad_t)


def solution(mesh):
    both = P("seg", "head")
    return jax.shard_map(
        per_device,
        mesh=mesh,
        in_specs=(both, both, both, both, P("head", None), P(), P()),
        out_specs=(both,) * 5,
        check_vma=False,
    )
```

```python
import functools
import math

import jax
import jax.numpy as jnp
from jax import lax
from jax.experimental import pallas as pl
from jax.experimental.pallas import tpu as pltpu
from jax.sharding import PartitionSpec as P

DH = 128
BLOCK = 128
F32 = jnp.float32
BF16 = jnp.bfloat16
HIDDEN = -1e30
VMEM = pl.BlockSpec(memory_space=pltpu.VMEM)
ANY = pl.BlockSpec(memory_space=pl.ANY)
HBM = pl.BlockSpec(memory_space=pltpu.HBM)
SMEM = pl.BlockSpec(memory_space=pltpu.SMEM)


def dot(left, right, dims):
    return lax.dot_general(left, right, ((dims[:1], dims[1:]), ((), ())), preferred_element_type=F32)


def lanes(block, width):
    return pl.ds(pl.multiple_of(block * width, width), width)


def call(body, outs, operands, specs=None, scratch=(), limit=20):
    return list(pl.pallas_call(
        body,
        out_shape=outs,
        in_specs=specs or [VMEM] * len(operands),
        out_specs=[VMEM] * len(outs),
        scratch_shapes=list(scratch),
        compiler_params=pltpu.CompilerParams(vmem_limit_bytes=limit * 2**20),
        cost_estimate=pl.CostEstimate(flops=1, bytes_accessed=1, transcendentals=0),
    )(*operands))


def shape(dims, dtype):
    return jax.ShapeDtypeStruct(dims, dtype)


def cut_body(A, B, k_ref, v_ref, *outs):
    a = lax.axis_index("seg") // B
    for m in range(A):
        head = lanes(a ^ m, DH)
        outs[m][:, :DH] = k_ref[:, head]
        outs[m][:, DH:] = v_ref[:, head]


def slope_body(A, B, H, *refs):
    grads, weight_ref, q_ref, outs, full, mixed = refs[:H], refs[H], refs[H + 1], refs[H + 2 : H + 2 + A], refs[-2], refs[-1]
    a = lax.axis_index("seg") // B
    h = lax.axis_index("head")
    width = grads[0].shape[1]
    for k in range(H):
        full[:, lanes(h ^ k, width)] = grads[k][...]
    mixed[...] = dot(full[...], weight_ref[...], (1, 1)).astype(BF16)
    for m in range(A):
        head = lanes(a ^ m, DH)
        outs[m][:, :DH] = q_ref[:, head]
        outs[m][:, DH : 2 * DH] = mixed[:, head]
        outs[m][:, 2 * DH :] = full[:, lanes((a ^ m) * H + h, width // H)]


def attend_body(A, B, R, score_scale, owner_ref, block_ref, *refs):
    pair = B == 2
    qdag_refs, refs = refs[:A], refs[A:]
    kv_refs, refs = (refs[: 2 * A], refs[2 * A :]) if pair else (refs[:1], refs[1:])
    attn_ref, dq_ref, own_ref, carry_ref, cot_ref, q_all, da_all, kv, kvcat = refs
    SEG = qdag_refs[0].shape[0]
    parts = SEG // BLOCK
    count = 2 * SEG + R * BLOCK
    seg = lax.axis_index("seg")
    a, b = seg // B, seg % B
    for m in range(A):
        q_all[m] = qdag_refs[m][:, :DH]
        da_all[m] = qdag_refs[m][:, DH : 2 * DH]
        cot_ref[m] = qdag_refs[m][:, 2 * DH :]
    if pair:
        for i in range(2 * A):
            for part in range(parts):
                kv[i * parts + part] = kv_refs[i][part * BLOCK : (part + 1) * BLOCK, :]
    else:
        kv = kv_refs[0]

    def place(other_a, other_b):
        slot = (other_b ^ b) * A + (other_a ^ a) if pair else other_b * A + (other_a ^ a)
        return slot * parts

    def segment(m):
        seg_a = a ^ m
        s = seg_a * B + b
        prev_b = jnp.where(b == 0, B - 1, b - 1)
        prev_a = jnp.where(b == 0, (seg_a + A - 1) % A, seg_a)
        column = lax.broadcasted_iota(jnp.int32, (1, count), 1)
        hidden = (column >= SEG) & (column < 2 * SEG) & (s == 0)
        for part in range(parts):
            at = part * BLOCK
            kvcat[at : at + BLOCK] = kv[place(seg_a, b) + part]
            kvcat[SEG + at : SEG + at + BLOCK] = kv[place(prev_a, prev_b) + part]
        for j in range(R):
            at = 2 * SEG + j * BLOCK
            owner, block = owner_ref[s, j], block_ref[s, j]
            kvcat[at : at + BLOCK] = kv[place(owner // B, owner % B) + jnp.maximum(block, 0)]
            hidden |= (column >= at) & (column < at + BLOCK) & (block < 0)
        bias = jnp.where(hidden, HIDDEN, 0.0)
        q, da = q_all[m], da_all[m]
        keys, values = kvcat[:, :DH], kvcat[:, DH:]
        scores = dot(q, keys, (1, 1)) * score_scale + bias
        row = lax.broadcasted_iota(jnp.int32, (SEG, SEG), 0)
        col = lax.broadcasted_iota(jnp.int32, (SEG, SEG), 1)
        scores = jnp.concatenate([jnp.where(row >= col, scores[:, :SEG], HIDDEN), scores[:, SEG:]], 1)
        top = jnp.max(scores, -1, keepdims=True)
        grown = jnp.exp(scores - top)
        weights = grown * (1.0 / jnp.sum(grown, -1, keepdims=True))
        rounded = weights.astype(BF16)
        attn = dot(rounded, values, (1, 0)).astype(BF16)
        attn_ref[m] = attn
        row_delta = jnp.sum(da.astype(F32) * attn.astype(F32), -1, keepdims=True)
        slopes = (weights * (dot(da, values, (1, 1)) - row_delta)).astype(BF16)
        dq_ref[m] = (score_scale * dot(slopes, keys, (1, 0))).astype(BF16)
        dk = score_scale * dot(slopes[:, : 2 * SEG], q, (0, 0))
        dv = dot(rounded[:, : 2 * SEG], da, (0, 0))
        own_ref[m, :, :DH] = dk[:SEG]
        own_ref[m, :, DH:] = dv[:SEG]
        slot = prev_a ^ a
        carry_ref[slot, :, :DH] = dk[SEG:].astype(BF16)
        carry_ref[slot, :, DH:] = dv[SEG:].astype(BF16)

    if pair:
        for m in range(A):
            segment(m)
    else:
        lax.fori_loop(0, A, lambda m, _: segment(m), None)


def project_body(A, B, H, *refs):
    attns, gs, weight_ref, refs = refs[:A], refs[A : A + H], refs[A + H], refs[A + H + 2 :]
    keep_ref, pass_ref, send_ref, *proj_refs = refs[:-3]
    own, mixed, cots = refs[-3:]
    seg = lax.axis_index("seg")
    a, b = seg // B, seg % B
    h = lax.axis_index("head")
    SEG = attns[0].shape[1]
    for m in range(A):
        head = lanes(a ^ m, DH)
        own[:, head] = attns[m][m]
        for i in range(A):
            mixed[(m ^ i) * SEG : (m ^ i) * SEG + SEG, head] = attns[m][i]
    width = keep_ref.shape[1]
    keep_ref[...] = dot(own[...], weight_ref[:, lanes(h, width)], (1, 0))
    pass_ref[...] = dot(own[...], weight_ref[:, lanes(h ^ 2, width)], (1, 0))
    for k in (1, 3):
        at = k // 2 * width
        send_ref[:, at : at + width] = dot(own[...], weight_ref[:, lanes(h ^ k, width)], (1, 0)).astype(BF16)
    piece = gs[0].shape[2]
    for k in range(H):
        for m in range(A):
            cots[m * SEG : (m + 1) * SEG, lanes(h ^ k, piece)] = gs[k][m]
    if B == 2:
        rows = piece * H // 2
        proj_refs[0][...] = dot(cots[:, lanes(b, rows)], mixed[...], (0, 0))
        proj_refs[1][...] = dot(cots[:, lanes(1 - b, rows)], mixed[...], (0, 0)).astype(BF16)
    else:
        proj_refs[0][...] = dot(cots[...], mixed[...], (0, 0))


def merge_body(A, dq_ref, own_ref, carry_ref, *outs):
    for m in range(A):
        outs[m][:, :DH] = dq_ref[m]
        outs[m][:, DH:] = (own_ref[m] + carry_ref[m].astype(F32)).astype(BF16)


def place_body(A, B, *refs):
    pieces, terms, projs, outs = refs[:A], refs[A : A + 3], refs[A + 3 : -5], refs[-5:]
    a = lax.axis_index("seg") // B
    for m in range(A):
        for i in range(3):
            outs[1 + i][:, lanes(a ^ m, DH)] = pieces[m][:, i * DH : (i + 1) * DH]
    outs[0][...] = sum(term[...].astype(F32) for term in terms).astype(BF16)
    outs[4][...] = sum(term[...].astype(F32) for term in projs)


def per_device(queries, keys, values, out_grad, out_weight, retr_owner, retr_block):
    n, H = lax.axis_size("seg"), lax.axis_size("head")
    SEG, width = queries.shape
    A = width // DH
    B = n // A
    R = retr_owner.shape[1]
    D = out_weight.shape[1]
    score_scale = 1.0 / math.sqrt(DH)

    def over_a(x, m):
        return lax.ppermute(x, "seg", [(i, (i // B ^ m) * B + i % B) for i in range(n)])

    def back_b(x):
        return lax.ppermute(x, "seg", [(i, i // B * B + (i % B - 1) % B) for i in range(n)])

    def over_head(x, k):
        return lax.ppermute(x, "head", [(i, i ^ k) for i in range(H)])

    def exchange(pieces):
        moved = {m: over_a(pieces[m], m) for m in reversed(range(1, A))}
        return [pieces[0]] + [moved[m] for m in range(1, A)]

    def direct(x):
        return [x] + [over_head(x, k) for k in range(1, H)]

    grads = direct(out_grad)
    cut = call(
        functools.partial(cut_body, A, B),
        [shape((SEG, 2 * DH), BF16)] * A,
        [keys, values],
        limit=60,
    )
    kvs = exchange(cut)
    sloped = call(
        functools.partial(slope_body, A, B, H),
        [shape((SEG, 2 * DH + width // H), BF16)] * A,
        [*grads, out_weight, queries],
        scratch=[pltpu.VMEM((SEG, D), BF16), pltpu.VMEM((SEG, width), BF16)],
    )
    if B == 2:
        sloped[0], *kvs = lax.optimization_barrier((sloped[0], *kvs))
        kvs = [*kvs, *(back_b(piece) for piece in kvs)]
    else:
        groups = [[i * B + j for j in range(B)] for i in range(A)]
        kvs = lax.all_gather(jnp.stack(kvs), "seg", axis_index_groups=groups)
        kvs = [kvs.reshape(B * A * (SEG // BLOCK), BLOCK, 2 * DH)]
    qdags = exchange(sloped)
    count = 2 * SEG + R * BLOCK
    attn, dq, own, carry, cot = call(
        functools.partial(attend_body, A, B, R, score_scale),
        [
            shape((A, SEG, DH), BF16),
            shape((A, SEG, DH), BF16),
            shape((A, SEG, 2 * DH), F32),
            shape((A, SEG, 2 * DH), BF16),
            shape((A, SEG, width // H), BF16),
        ],
        [retr_owner, retr_block, *qdags, *kvs],
        specs=[SMEM] * 2 + [VMEM] * (A + len(kvs)),
        scratch=[
            pltpu.VMEM((A, SEG, DH), BF16),
            pltpu.VMEM((A, SEG, DH), BF16),
            pltpu.VMEM((2 * A * (SEG // BLOCK), BLOCK, 2 * DH), BF16),
            pltpu.VMEM((count, 2 * DH), BF16),
        ],
    )
    attns = exchange([attn] * A)
    carried = back_b(carry)
    gs = direct(cot)
    merged = call(
        functools.partial(merge_body, A), [shape((SEG, 3 * DH), BF16)] * A, [dq, own, carried]
    )
    partials = [shape((SEG, D // H), F32)] * 2 + [shape((SEG, D // 2), BF16)]
    rows = D // A
    if B == 2:
        projs = [shape((rows // 2, width), F32), shape((rows // 2, width), BF16)]
    else:
        projs = [shape((rows, width), F32)]
    keep, passed, send, *proj = call(
        functools.partial(project_body, A, B, H),
        partials + projs,
        [*attns, *gs, out_weight, merged[0]],
        specs=[VMEM] * (A + H + 1) + [ANY],
        scratch=[
            pltpu.VMEM((SEG, width), BF16),
            pltpu.VMEM((A * SEG, width), BF16),
            pltpu.VMEM((A * SEG, rows), BF16),
        ],
    )
    moved = exchange(merged)
    block = D // H
    received = over_head(send, 1)
    passed = (passed + received[:, block:].astype(F32)).astype(BF16)
    if B == 2:
        proj = [proj[0], back_b(proj[1])]
    else:
        proj = [lax.psum_scatter(proj[0], "seg", scatter_dimension=0, axis_index_groups=groups, tiled=True)]
    return tuple(
        call(
            functools.partial(place_body, A, B),
            [shape((SEG, width), BF16)] * 4 + [shape(proj[0].shape, F32)],
            [*moved, keep, received[:, :block], over_head(passed, 2), *proj],
        )
    )


def solution(mesh):
    both = P("seg", "head")
    return jax.shard_map(
        per_device,
        mesh=mesh,
        in_specs=(both, both, both, both, P("head", None), P(), P()),
        out_specs=(both,) * 5,
        check_vma=False,
    )
```

```python
import functools
import math

import jax
import jax.numpy as jnp
from jax import lax
from jax.experimental import pallas as pl
from jax.experimental.pallas import tpu as pltpu
from jax.sharding import PartitionSpec as P

DH = 128
BLOCK = 128
F32 = jnp.float32
BF16 = jnp.bfloat16
HIDDEN = -1e30
VMEM = pl.BlockSpec(memory_space=pltpu.VMEM)
ANY = pl.BlockSpec(memory_space=pl.ANY)
HBM = pl.BlockSpec(memory_space=pltpu.HBM)
SMEM = pl.BlockSpec(memory_space=pltpu.SMEM)


def dot(left, right, dims):
    return lax.dot_general(left, right, ((dims[:1], dims[1:]), ((), ())), preferred_element_type=F32)


def lanes(block, width):
    return pl.ds(pl.multiple_of(block * width, width), width)


def call(body, outs, operands, specs=None, scratch=(), limit=20):
    return list(pl.pallas_call(
        body,
        out_shape=outs,
        in_specs=specs or [VMEM] * len(operands),
        out_specs=[VMEM] * len(outs),
        scratch_shapes=list(scratch),
        compiler_params=pltpu.CompilerParams(vmem_limit_bytes=limit * 2**20),
        cost_estimate=pl.CostEstimate(flops=1, bytes_accessed=1, transcendentals=0),
    )(*operands))


def shape(dims, dtype):
    return jax.ShapeDtypeStruct(dims, dtype)


def cut_body(A, B, k_ref, v_ref, *outs):
    a = lax.axis_index("seg") % A
    for m in range(A):
        head = lanes(a ^ m, DH)
        outs[m][:, :DH] = k_ref[:, head]
        outs[m][:, DH:] = v_ref[:, head]


def cot_piece(full, A, B, other, half):
    total = full.shape[1]
    part, own = total // (A * 2), total // (A * B)
    if own == part:
        return full[:, lanes(half * A + other, part)]
    row = lax.broadcasted_iota(jnp.int32, (part * A, part), 0)
    col = lax.broadcasted_iota(jnp.int32, (part * A, part), 1)
    pick = (row == (col // own * A + other) * own + col % own).astype(BF16)
    return dot(full[:, lanes(half, part * A)], pick, (1, 0)).astype(BF16)


def slope_body(A, B, H, *refs):
    grads, weight_ref, q_ref, refs = refs[:H], refs[H], refs[H + 1], refs[H + 2 :]
    outs, full, mixed = refs[:A], refs[-2], refs[-1]
    a = lax.axis_index("seg") % A
    h = lax.axis_index("head")
    width = grads[0].shape[1]
    for k in range(H):
        full[:, lanes(h ^ k, width)] = grads[k][...]
    mixed[...] = dot(full[...], weight_ref[...], (1, 1)).astype(BF16)
    for m in range(A):
        head = lanes(a ^ m, DH)
        outs[m][:, :DH] = q_ref[:, head]
        outs[m][:, DH : 2 * DH] = mixed[:, head]
        outs[m][:, 2 * DH :] = cot_piece(full, A, B, a ^ m, h % 2)


def pack_body(A, *refs):
    for m in range(A):
        refs[A + m // (A - 1)][m % (A - 1)] = refs[m][...]


def attend_body(A, B, R, score_scale, owner_ref, block_ref, *refs):
    pair = B == 2
    piece_refs, own_refs, others, refs = refs[:A], refs[A : 2 * A], refs[2 * A : -10], refs[-10:]
    attn_ref, dq_ref, own_ref, cache_ref, carry_ref, cot_ref, q_all, da_all, kv, kvcat = refs
    SEG = piece_refs[0].shape[0]
    parts = SEG // BLOCK
    count = 2 * SEG + R * BLOCK
    seg = lax.axis_index("seg")
    a, b = seg % A, seg // A
    for m in range(A):
        q_all[m] = piece_refs[m][:, :DH]
        da_all[m] = piece_refs[m][:, DH : 2 * DH]
        cot_ref[m] = piece_refs[m][:, 2 * DH :]
    if pair:
        for m in range(A):
            for part in range(parts):
                rows = slice(part * BLOCK, (part + 1) * BLOCK)
                kv[m * parts + part] = own_refs[m][rows, :]
                kv[(A + m) * parts + part] = others[m // (A - 1)][m % (A - 1), rows, :]
    else:
        kv = others[0]

    def place(other_a, other_b):
        slot = (other_b ^ b) * A + (other_a ^ a) if pair else other_b * A + (other_a ^ a)
        return slot * parts

    def segment(m):
        seg_a = a ^ m
        s = b * A + seg_a
        prev_a = jnp.where(seg_a == 0, A - 1, seg_a - 1)
        prev_b = jnp.where(seg_a == 0, (b + B - 1) % B, b)
        far = count - SEG
        column = lax.broadcasted_iota(jnp.int32, (1, far), 1)
        hidden = (column < SEG) & (s == 0)
        for part in range(parts):
            at = part * BLOCK
            kvcat[at : at + BLOCK] = kv[place(seg_a, b) + part]
            kvcat[SEG + at : SEG + at + BLOCK] = kv[place(prev_a, prev_b) + part]
        for j in range(R):
            at = SEG + j * BLOCK
            owner, block = owner_ref[s, j], block_ref[s, j]
            kvcat[SEG + at : SEG + at + BLOCK] = kv[place(owner % A, owner // A) + jnp.maximum(block, 0)]
            hidden |= (column >= at) & (column < at + BLOCK) & (block < 0)
        bias = jnp.where(hidden, HIDDEN, 0.0)
        q, da = q_all[m], da_all[m]
        keys, values = kvcat[:, :DH], kvcat[:, DH:]
        near_keys, far_keys, near_values, far_values = keys[:SEG], keys[SEG:], values[:SEG], values[SEG:]
        row = lax.broadcasted_iota(jnp.int32, (SEG, SEG), 0)
        col = lax.broadcasted_iota(jnp.int32, (SEG, SEG), 1)
        scale = score_scale * math.log2(math.e)
        near = jnp.where(row >= col, dot(q, near_keys, (1, 1)) * scale, HIDDEN)
        rest = dot(q, far_keys, (1, 1)) * scale + bias
        top = jnp.maximum(jnp.max(near, -1, keepdims=True), jnp.max(rest, -1, keepdims=True))
        near, rest = jnp.exp2(near - top), jnp.exp2(rest - top)
        inverse = 1.0 / (jnp.sum(near, -1, keepdims=True) + jnp.sum(rest, -1, keepdims=True))
        near, rest = near * inverse, rest * inverse
        near_rounded, rounded = near.astype(BF16), rest.astype(BF16)
        attn = (dot(near_rounded, near_values, (1, 0)) + dot(rounded, far_values, (1, 0))).astype(BF16)
        attn_ref[m] = attn
        row_delta = jnp.sum(da.astype(F32) * attn.astype(F32), -1, keepdims=True)
        near_slopes = (near * (dot(da, near_values, (1, 1)) - row_delta)).astype(BF16)
        slopes = (rest * (dot(da, far_values, (1, 1)) - row_delta)).astype(BF16)
        dq_ref[m] = (score_scale * (dot(near_slopes, near_keys, (1, 0)) + dot(slopes, far_keys, (1, 0)))).astype(BF16)
        own_ref[m, :, :DH] = score_scale * dot(near_slopes, q, (0, 0))
        own_ref[m, :, DH:] = dot(near_rounded, da, (0, 0))
        dk = (score_scale * dot(slopes[:, :SEG], q, (0, 0))).astype(BF16)
        dv = dot(rounded[:, :SEG], da, (0, 0)).astype(BF16)
        cache_ref[prev_a ^ a, :, :DH] = dk
        cache_ref[prev_a ^ a, :, DH:] = dv

        @pl.when(seg_a == 0)
        def _():
            carry_ref[:, :DH] = dk
            carry_ref[:, DH:] = dv

    if pair:
        for m in range(A):
            segment(m)
    else:
        lax.fori_loop(0, A, lambda m, _: segment(m), None)


def project_body(A, B, H, *refs):
    attns, gs, weight_ref, refs = refs[:A], refs[A : A + 2], refs[A + 2], refs[A + 4 :]
    keep_ref, pass_ref, send_ref, *proj_refs = refs[:-3]
    own, mixed, cots = refs[-3:]
    seg = lax.axis_index("seg")
    a, b = seg % A, seg // A
    h = lax.axis_index("head")
    SEG = attns[0].shape[1]
    for m in range(A):
        head = lanes(a ^ m, DH)
        own[:, head] = attns[m][m]
        for i in range(A):
            mixed[(m ^ i) * SEG : (m ^ i) * SEG + SEG, head] = attns[m][i]
    width = keep_ref.shape[1]
    keep_ref[...] = dot(own[...], weight_ref[:, lanes(h, width)], (1, 0))
    pass_ref[...] = dot(own[...], weight_ref[:, lanes(h ^ 2, width)], (1, 0))
    for k in (1, 3):
        at = k // 2 * width
        send_ref[:, at : at + width] = dot(own[...], weight_ref[:, lanes(h ^ k, width)], (1, 0)).astype(BF16)
    piece = gs[0].shape[2]
    for k in range(2):
        for m in range(A):
            cots[m * SEG : (m + 1) * SEG, lanes(h % 2 ^ k, piece)] = gs[k][m]
    if B == 2:
        rows = piece
        proj_refs[0][...] = dot(cots[:, lanes(b, rows)], mixed[...], (0, 0))
        proj_refs[1][...] = dot(cots[:, lanes(1 - b, rows)], mixed[...], (0, 0)).astype(BF16)
    else:
        proj_refs[0][...] = dot(cots[...], mixed[...], (0, 0))


def merge_body(A, dq_ref, own_ref, cache_ref, carry_ref, *outs):
    a = lax.axis_index("seg") % A
    for m in range(A):
        outs[m][:, :DH] = dq_ref[m]
        late = jnp.where(a ^ m == A - 1, carry_ref[...], cache_ref[m])
        outs[m][:, DH:] = (own_ref[m] + late.astype(F32)).astype(BF16)


def place_body(A, B, *refs):
    pieces, terms, projs, outs = refs[:A], refs[A : A + 3], refs[A + 3 : -5], refs[-5:]
    a = lax.axis_index("seg") % A
    for m in range(A):
        for i in range(3):
            outs[1 + i][:, lanes(a ^ m, DH)] = pieces[m][:, i * DH : (i + 1) * DH]
    outs[0][...] = sum(term[...].astype(F32) for term in terms).astype(BF16)
    outs[4][...] = sum(term[...].astype(F32) for term in projs)


def per_device(queries, keys, values, out_grad, out_weight, retr_owner, retr_block):
    n, H = lax.axis_size("seg"), lax.axis_size("head")
    SEG, width = queries.shape
    A = width // DH
    B = n // A
    R = retr_owner.shape[1]
    D = out_weight.shape[1]
    score_scale = 1.0 / math.sqrt(DH)

    def over_a(x, m):
        return lax.ppermute(x, "seg", [(i, i // A * A + (i % A ^ m)) for i in range(n)])

    def over_b(x):
        return lax.ppermute(x, "seg", [(i, (i + A) % n) for i in range(n)])

    def back_b(x):
        return lax.ppermute(x, "seg", [(i, i - A) for i in range(A, n)])

    def over_head(x, k):
        return lax.ppermute(x, "head", [(i, i ^ k) for i in range(H)])

    def exchange(pieces):
        moved = {m: over_a(pieces[m], m) for m in reversed(range(1, A))}
        return [pieces[0]] + [moved[m] for m in range(1, A)]

    def direct(x):
        return [x] + [over_head(x, k) for k in range(1, H)]

    grads = direct(out_grad)

    cut = functools.partial(cut_body, A, B)
    kvs = exchange(call(cut, [shape((SEG, 2 * DH), BF16)] * A, [keys, values]))
    kv = call(
        functools.partial(pack_body, A), [shape((A - 1, SEG, 2 * DH), BF16), shape((1, SEG, 2 * DH), BF16)], kvs
    )
    if B == 2:
        kv = [over_b(piece) for piece in kv]
    else:
        groups = [[j * A + i for j in range(B)] for i in range(A)]
        kv = lax.all_gather(jnp.concatenate(kv), "seg", axis_index_groups=groups)
        kv = [kv.reshape(B * A * (SEG // BLOCK), BLOCK, 2 * DH)]
    sloped = call(
        functools.partial(slope_body, A, B, H),
        [shape((SEG, 2 * DH + width // 2), BF16)] * A,
        [*grads, out_weight, queries],
        scratch=[pltpu.VMEM((SEG, D), BF16), pltpu.VMEM((SEG, width), BF16)],
    )
    pieces = exchange(sloped)
    count = 2 * SEG + R * BLOCK
    attn, dq, own, cache, carry, cot = call(
        functools.partial(attend_body, A, B, R, score_scale),
        [
            shape((A, SEG, DH), BF16),
            shape((A, SEG, DH), BF16),
            shape((A, SEG, 2 * DH), F32),
            shape((A, SEG, 2 * DH), BF16),
            shape((SEG, 2 * DH), BF16),
            shape((A, SEG, width // 2), BF16),
        ],
        [retr_owner, retr_block, *pieces, *kvs, *kv],
        specs=[SMEM] * 2 + [VMEM] * (2 * A + len(kv)),
        scratch=[
            pltpu.VMEM((A, SEG, DH), BF16),
            pltpu.VMEM((A, SEG, DH), BF16),
            pltpu.VMEM((2 * A * (SEG // BLOCK), BLOCK, 2 * DH), BF16),
            pltpu.VMEM((count, 2 * DH), BF16),
        ],
    )
    attns = exchange([attn] * A)
    carried = back_b(carry)
    gs = [cot, over_head(cot, 1)]
    merged = call(
        functools.partial(merge_body, A), [shape((SEG, 3 * DH), BF16)] * A, [dq, own, cache, carried]
    )
    partials = [shape((SEG, D // H), F32)] * 2 + [shape((SEG, D // 2), BF16)]
    rows = D // A
    if B == 2:
        projs = [shape((rows // 2, width), F32), shape((rows // 2, width), BF16)]
    else:
        projs = [shape((rows, width), F32)]
    keep, passed, send, *proj = call(
        functools.partial(project_body, A, B, H),
        partials + projs,
        [*attns, *gs, out_weight, merged[0]],
        specs=[VMEM] * (A + 3) + [ANY],
        scratch=[
            pltpu.VMEM((SEG, width), BF16),
            pltpu.VMEM((A * SEG, width), BF16),
            pltpu.VMEM((A * SEG, rows), BF16),
        ],
    )
    moved = exchange(merged)
    block = D // H
    received = over_head(send, 1)
    passed = (passed + received[:, block:].astype(F32)).astype(BF16)
    if B == 2:
        proj = [proj[0], over_b(proj[1])]
    else:
        proj = [lax.psum_scatter(proj[0], "seg", scatter_dimension=0, axis_index_groups=groups, tiled=True)]
    return tuple(
        call(
            functools.partial(place_body, A, B),
            [shape((SEG, width), BF16)] * 4 + [shape(proj[0].shape, F32)],
            [*moved, keep, received[:, :block], over_head(passed, 2), *proj],
        )
    )


def solution(mesh):
    both = P("seg", "head")
    return jax.shard_map(
        per_device,
        mesh=mesh,
        in_specs=(both, both, both, both, P("head", None), P(), P()),
        out_specs=(both,) * 5,
        check_vma=False,
    )
```

```python
import functools
import math

import jax
import jax.numpy as jnp
from jax import lax
from jax.experimental import pallas as pl
from jax.experimental.pallas import tpu as pltpu
from jax.sharding import PartitionSpec as P

DH = 128
BLOCK = 128
F32 = jnp.float32
BF16 = jnp.bfloat16
HIDDEN = -1e30
VMEM = pl.BlockSpec(memory_space=pltpu.VMEM)
ANY = pl.BlockSpec(memory_space=pl.ANY)
HBM = pl.BlockSpec(memory_space=pltpu.HBM)
SMEM = pl.BlockSpec(memory_space=pltpu.SMEM)


def dot(left, right, dims):
    return lax.dot_general(left, right, ((dims[:1], dims[1:]), ((), ())), preferred_element_type=F32)


def lanes(block, width):
    return pl.ds(pl.multiple_of(block * width, width), width)


def call(body, outs, operands, specs=None, scratch=(), limit=20, flops=1):
    return list(pl.pallas_call(
        body,
        out_shape=outs,
        in_specs=specs or [VMEM] * len(operands),
        out_specs=[VMEM] * len(outs),
        scratch_shapes=list(scratch),
        compiler_params=pltpu.CompilerParams(vmem_limit_bytes=limit * 2**20),
        cost_estimate=pl.CostEstimate(flops=flops, bytes_accessed=1, transcendentals=0),
    )(*operands))


def shape(dims, dtype):
    return jax.ShapeDtypeStruct(dims, dtype)


def cut_body(A, B, k_ref, v_ref, *outs):
    a = lax.axis_index("seg") % A
    for m in range(A):
        head = lanes(a ^ m, DH)
        outs[m][:, :DH] = k_ref[:, head]
        outs[m][:, DH:] = v_ref[:, head]


def cot_piece(full, A, B, H, other, h):
    total = full.shape[1]
    part, own = total // (A * H), total // (A * B)
    if own % part == 0:
        split = own // part
        return full[:, lanes(((h // split) * A + other) * split + h % split, part)]
    row = lax.broadcasted_iota(jnp.int32, (part * A, part), 0)
    col = lax.broadcasted_iota(jnp.int32, (part * A, part), 1)
    pick = (row == (col // own * A + other) * own + col % own).astype(BF16)
    return dot(full[:, lanes(h, part * A)], pick, (1, 0)).astype(BF16)


def slope_body(A, B, H, *refs):
    grads, weight_ref, q_ref, refs = refs[:H], refs[H], refs[H + 1], refs[H + 2 :]
    outs, full, mixed = refs[:A], refs[-2], refs[-1]
    a = lax.axis_index("seg") % A
    h = lax.axis_index("head")
    width = grads[0].shape[1]
    for k in range(H):
        full[:, lanes(h ^ k, width)] = grads[k][...]
    mixed[...] = dot(full[...], weight_ref[...], (1, 1)).astype(BF16)
    for m in range(A):
        head = lanes(a ^ m, DH)
        outs[m][:, :DH] = q_ref[:, head]
        outs[m][:, DH : 2 * DH] = mixed[:, head]
        outs[m][:, 2 * DH :] = cot_piece(full, A, B, H, a ^ m, h)


def pack_body(A, *refs):
    for m in range(A):
        refs[-1][A - 1 - m] = refs[m][...]


def collect_body(*refs):
    for m, ref in enumerate(refs[:-1]):
        refs[-1][m] = ref[:, 2 * DH :]


def join_body(*refs):
    for i, ref in enumerate(refs[:-1]):
        refs[-1][i] = ref[...]


def stage_body(*refs):
    half = len(refs) // 2
    for source, target in zip(refs[:half], refs[half:]):
        target[...] = source[...]


def forward_body(A, B, R, score_scale, owner_ref, block_ref, *refs):
    pair = B == 2
    piece_refs, own_refs, other_ref, refs = refs[:A][::-1], refs[A : 2 * A], refs[2 * A], refs[2 * A + 1 :]
    attn_ref, kvcat, weights_ref, kv = refs
    SEG = piece_refs[0].shape[0]
    parts = SEG // BLOCK
    count = 2 * SEG + R * BLOCK
    seg = lax.axis_index("seg")
    a, b = seg % A, seg // A
    if pair:
        for m in range(A):
            for part in range(parts):
                rows = slice(part * BLOCK, (part + 1) * BLOCK)
                kv[m * parts + part] = own_refs[m][rows, :]
                kv[(A + m) * parts + part] = other_ref[m, rows, :]
    else:
        kv = other_ref

    def place(other_a, other_b):
        slot = (other_b ^ b) * A + (other_a ^ a) if pair else other_b * A + (other_a ^ a)
        return slot * parts

    for m in range(A):
        seg_a = a ^ m
        s = b * A + seg_a
        prev_a = jnp.where(seg_a == 0, A - 1, seg_a - 1)
        prev_b = jnp.where(seg_a == 0, (b + B - 1) % B, b)
        far = count - SEG
        column = lax.broadcasted_iota(jnp.int32, (1, far), 1)
        hidden = (column < SEG) & (s == 0)
        for part in range(parts):
            at = part * BLOCK
            kvcat[m, at : at + BLOCK] = kv[place(seg_a, b) + part]
            kvcat[m, SEG + at : SEG + at + BLOCK] = kv[place(prev_a, prev_b) + part]
        for j in range(R):
            at = SEG + j * BLOCK
            owner, block = owner_ref[s, j], block_ref[s, j]
            kvcat[m, SEG + at : SEG + at + BLOCK] = kv[place(owner % A, owner // A) + jnp.maximum(block, 0)]
            hidden |= (column >= at) & (column < at + BLOCK) & (block < 0)
        bias = jnp.where(hidden, HIDDEN, 0.0)
        q = piece_refs[m][:, :DH]
        row = lax.broadcasted_iota(jnp.int32, (SEG, SEG), 0)
        col = lax.broadcasted_iota(jnp.int32, (SEG, SEG), 1)
        scale = score_scale * math.log2(math.e)
        near = jnp.where(row >= col, dot(q, kvcat[m, :SEG, :DH], (1, 1)) * scale, HIDDEN)
        rest = dot(q, kvcat[m, SEG:, :DH], (1, 1)) * scale + bias
        top = jnp.maximum(jnp.max(near, -1, keepdims=True), jnp.max(rest, -1, keepdims=True))
        near, rest = jnp.exp2(near - top), jnp.exp2(rest - top)
        inverse = 1.0 / (jnp.sum(near, -1, keepdims=True) + jnp.sum(rest, -1, keepdims=True))
        near, rest = near * inverse, rest * inverse
        weights_ref[m, :, :SEG] = near.astype(weights_ref.dtype)
        weights_ref[m, :, SEG:] = rest.astype(weights_ref.dtype)
        near, rest = near.astype(BF16), rest.astype(BF16)
        attn_ref[m] = (dot(near, kvcat[m, :SEG, DH:], (1, 0)) + dot(rest, kvcat[m, SEG:, DH:], (1, 0))).astype(BF16)


def backward_body(A, B, score_scale, attn_ref, kvcat, weights_ref, *refs):
    piece_refs, (dq_ref, own_ref, cache_ref, carry_ref) = refs[:A], refs[A:]
    SEG = piece_refs[0].shape[0]
    a = lax.axis_index("seg") % A
    for m in range(A):
        seg_a = a ^ m
        prev_a = jnp.where(seg_a == 0, A - 1, seg_a - 1)
        q, da = piece_refs[m][:, :DH], piece_refs[m][:, DH : 2 * DH]
        row_delta = jnp.sum(da.astype(F32) * attn_ref[m].astype(F32), -1, keepdims=True)
        weights = weights_ref[m]
        rounded = weights.astype(BF16)
        slopes = (weights.astype(F32) * (dot(da, kvcat[m, :, DH:], (1, 1)) - row_delta)).astype(BF16)
        dq_ref[m] = (score_scale * dot(slopes, kvcat[m, :, :DH], (1, 0))).astype(BF16)
        dk = score_scale * dot(slopes[:, : 2 * SEG], q, (0, 0))
        dv = dot(rounded[:, : 2 * SEG], da, (0, 0))
        own_ref[m, :, :DH] = dk[:SEG]
        own_ref[m, :, DH:] = dv[:SEG]
        dk, dv = dk[SEG:].astype(BF16), dv[SEG:].astype(BF16)
        cache_ref[prev_a ^ a, :, :DH] = dk
        cache_ref[prev_a ^ a, :, DH:] = dv

        @pl.when(seg_a == 0)
        def _():
            carry_ref[:, :DH] = dk
            carry_ref[:, DH:] = dv


def project_body(A, B, H, *refs):
    attns, gs, weight_ref, refs = refs[:A][::-1], refs[A : A + 2], refs[A + 2], refs[A + 4 :]
    keep_ref, pass_ref, send_ref, *proj_refs = refs[:-3]
    own, mixed, cots = refs[-3:]
    seg = lax.axis_index("seg")
    a, b = seg % A, seg // A
    h = lax.axis_index("head")
    SEG = attns[0].shape[1]
    for m in range(A):
        head = lanes(a ^ m, DH)
        own[:, head] = attns[m][m]
        for i in range(A):
            mixed[(m ^ i) * SEG : (m ^ i) * SEG + SEG, head] = attns[m][i]
    width = keep_ref.shape[1]
    keep_ref[...] = dot(own[...], weight_ref[:, lanes(h, width)], (1, 0))
    pass_ref[...] = dot(own[...], weight_ref[:, lanes(h ^ 2, width)], (1, 0))
    for k in (1, 3):
        at = k // 2 * width
        send_ref[:, at : at + width] = dot(own[...], weight_ref[:, lanes(h ^ k, width)], (1, 0)).astype(BF16)
    piece = gs[0].shape[3]
    for k in range(H):
        for m in range(A):
            cots[m * SEG : (m + 1) * SEG, lanes(h ^ k, piece)] = gs[k % 2][k // 2, m]
    if B == 2:
        rows = piece * H // 2
        proj_refs[0][...] = dot(cots[:, lanes(b, rows)], mixed[...], (0, 0))
        proj_refs[1][...] = dot(cots[:, lanes(1 - b, rows)], mixed[...], (0, 0)).astype(BF16)
    else:
        proj_refs[0][...] = dot(cots[...], mixed[...], (0, 0))


def merge_body(A, dq_ref, own_ref, cache_ref, carry_ref, *outs):
    a = lax.axis_index("seg") % A
    for m in range(A):
        outs[m][:, :DH] = dq_ref[m]
        late = jnp.where(a ^ m == A - 1, carry_ref[...], cache_ref[m])
        outs[m][:, DH:] = (own_ref[m] + late.astype(F32)).astype(BF16)


def place_body(A, B, *refs):
    pieces, projs, outs = refs[:A][::-1], refs[A:-4], refs[-4:]
    a = lax.axis_index("seg") % A
    for m in range(A):
        for i in range(3):
            outs[i][:, lanes(a ^ m, DH)] = pieces[m][:, i * DH : (i + 1) * DH]
    outs[3][...] = sum(term[...].astype(F32) for term in projs)


def per_device(queries, keys, values, out_grad, out_weight, retr_owner, retr_block):
    n, H = lax.axis_size("seg"), lax.axis_size("head")
    SEG, width = queries.shape
    A = width // DH
    B = n // A
    R = retr_owner.shape[1]
    D = out_weight.shape[1]
    score_scale = 1.0 / math.sqrt(DH)

    def over_a(x, m):
        return lax.ppermute(x, "seg", [(i, i // A * A + (i % A ^ m)) for i in range(n)])

    def over_b(x):
        return lax.ppermute(x, "seg", [(i, (i + A) % n) for i in range(n)])

    def back_b(x):
        return lax.ppermute(x, "seg", [(i, i - A) for i in range(A, n)])

    def over_head(x, k):
        return lax.ppermute(x, "head", [(i, i ^ k) for i in range(H)])

    def exchange(pieces):
        moved = {m: over_a(pieces[m], m) for m in reversed(range(1, A))}
        return [pieces[0]] + [moved[m] for m in range(1, A)]

    def direct(x):
        return [x] + [over_head(x, k) for k in range(1, H)]

    grads = direct(out_grad)

    cut = functools.partial(cut_body, A, B)
    kvs = exchange(call(cut, [shape((SEG, 2 * DH), BF16)] * A, [keys, values]))
    staged = call(stage_body, [shape(x.shape, BF16) for x in (out_weight, queries, out_grad)], [out_weight, queries, out_grad])
    kv = call(
        functools.partial(pack_body, A),
        [shape((A, SEG, 2 * DH), BF16)],
        [*kvs[::-1], staged[0]],
        specs=[VMEM] * A + [ANY],
    )[0]
    out_weight, queries, grads[0] = staged
    if B == 2:
        kv = over_b(kv)
    else:
        groups = [[j * A + i for j in range(B)] for i in range(A)]
        kv = lax.all_gather(kv, "seg", axis_index_groups=groups)
        kv = kv.reshape(B * A * (SEG // BLOCK), BLOCK, 2 * DH)
    sloped = call(
        functools.partial(slope_body, A, B, H),
        [shape((SEG, 2 * DH + width // H), BF16)] * A,
        [*grads, out_weight, queries],
        scratch=[pltpu.VMEM((SEG, D), BF16), pltpu.VMEM((SEG, width), BF16)],
        flops=10**9,
    )
    pieces = exchange(sloped)
    count = 2 * SEG + R * BLOCK
    cot = call(collect_body, [shape((A, SEG, width // H), BF16)], pieces)[0]
    far_cot = over_head(cot, 2)
    limit = 20 if B == 2 else 60
    attn, kvcat, weights = call(
        functools.partial(forward_body, A, B, R, score_scale),
        [shape((A, SEG, DH), BF16), shape((A, count, 2 * DH), BF16), shape((A, SEG, count), F32)],
        [retr_owner, retr_block, *pieces[::-1], *kvs, kv],
        specs=[SMEM] * 2 + [VMEM] * (2 * A + 1),
        scratch=[pltpu.VMEM((2 * A * (SEG // BLOCK), BLOCK, 2 * DH), BF16)],
        limit=limit,
        flops=10**11,
    )
    dq, own, cache, carry = call(
        functools.partial(backward_body, A, B, score_scale),
        [
            shape((A, SEG, DH), BF16),
            shape((A, SEG, 2 * DH), F32),
            shape((A, SEG, 2 * DH), BF16),
            shape((SEG, 2 * DH), BF16),
        ],
        [attn, kvcat, weights, *pieces],
        limit=limit,
        flops=10**11,
    )
    attns = exchange([attn] * A)
    carried = back_b(carry)
    cots = call(join_body, [shape((2, *cot.shape), BF16)], [cot, far_cot])[0]
    gs = [cots, over_head(cots, 1)]
    merged = call(
        functools.partial(merge_body, A), [shape((SEG, 3 * DH), BF16)] * A, [dq, own, cache, carried]
    )
    partials = [shape((SEG, D // H), F32)] * 2 + [shape((SEG, D // 2), BF16)]
    rows = D // A
    if B == 2:
        projs = [shape((rows // 2, width), F32), shape((rows // 2, width), BF16)]
    else:
        projs = [shape((rows, width), F32)]
    keep, passed, send, *proj = call(
        functools.partial(project_body, A, B, H),
        partials + projs,
        [*attns[::-1], *gs, out_weight, merged[0]],
        specs=[VMEM] * (A + 3) + [ANY],
        scratch=[
            pltpu.VMEM((SEG, width), BF16),
            pltpu.VMEM((A * SEG, width), BF16),
            pltpu.VMEM((A * SEG, rows), BF16),
        ],
    )
    moved = exchange(merged)
    block = D // H
    received = over_head(send, 1)
    passed = (passed + received[:, block:].astype(F32)).astype(BF16)
    if B == 2:
        proj = [proj[0], over_b(proj[1])]
    else:
        proj = [lax.psum_scatter(proj[0], "seg", scatter_dimension=0, axis_index_groups=groups, tiled=True)]
    *placed, proj_grad_t = call(
        functools.partial(place_body, A, B),
        [shape((SEG, width), BF16)] * 3 + [shape(proj[0].shape, F32)],
        [*moved[::-1], *proj],
        flops=10**11,
    )
    placed[0], keep = lax.optimization_barrier((placed[0], keep))
    layer_out = keep + received[:, :block].astype(F32) + over_head(passed, 2).astype(F32)
    return (layer_out.astype(BF16), *placed, proj_grad_t)


def solution(mesh):
    both = P("seg", "head")
    return jax.shard_map(
        per_device,
        mesh=mesh,
        in_specs=(both, both, both, both, P("head", None), P(), P()),
        out_specs=(both,) * 5,
        check_vma=False,
    )
```

```python
import functools
import math

import jax
import jax.numpy as jnp
from jax import lax
from jax.experimental import pallas as pl
from jax.experimental.pallas import tpu as pltpu
from jax.sharding import PartitionSpec as P

DH = 128
BLOCK = 128
F32 = jnp.float32
BF16 = jnp.bfloat16
HIDDEN = -1e30
VMEM = pl.BlockSpec(memory_space=pltpu.VMEM)
ANY = pl.BlockSpec(memory_space=pl.ANY)
HBM = pl.BlockSpec(memory_space=pltpu.HBM)
SMEM = pl.BlockSpec(memory_space=pltpu.SMEM)


def dot(left, right, dims):
    return lax.dot_general(left, right, ((dims[:1], dims[1:]), ((), ())), preferred_element_type=F32)


def lanes(block, width):
    return pl.ds(pl.multiple_of(block * width, width), width)


def call(body, outs, operands, specs=None, scratch=(), limit=20, flops=1):
    return list(pl.pallas_call(
        body,
        out_shape=outs,
        in_specs=specs or [VMEM] * len(operands),
        out_specs=[VMEM] * len(outs),
        scratch_shapes=list(scratch),
        compiler_params=pltpu.CompilerParams(vmem_limit_bytes=limit * 2**20),
        cost_estimate=pl.CostEstimate(flops=flops, bytes_accessed=1, transcendentals=0),
    )(*operands))


def shape(dims, dtype):
    return jax.ShapeDtypeStruct(dims, dtype)


def cut_body(A, B, k_ref, v_ref, *outs):
    a = lax.axis_index("seg") % A
    for m in range(A):
        head = lanes(a ^ m, DH)
        outs[m][:, :DH] = k_ref[:, head]
        outs[m][:, DH:] = v_ref[:, head]


def cot_piece(full, A, B, H, other, h):
    total = full.shape[1]
    part, own = total // (A * H), total // (A * B)
    if own % part == 0:
        split = own // part
        return full[:, lanes(((h // split) * A + other) * split + h % split, part)]
    row = lax.broadcasted_iota(jnp.int32, (part * A, part), 0)
    col = lax.broadcasted_iota(jnp.int32, (part * A, part), 1)
    pick = (row == (col // own * A + other) * own + col % own).astype(BF16)
    return dot(full[:, lanes(h, part * A)], pick, (1, 0)).astype(BF16)


def slope_body(A, B, H, *refs):
    grads, weight_ref, q_ref, refs = refs[:H], refs[H], refs[H + 1], refs[H + 2 :]
    outs, full, mixed = refs[:A], refs[-2], refs[-1]
    a = lax.axis_index("seg") % A
    h = lax.axis_index("head")
    width = grads[0].shape[1]
    for k in range(H):
        full[:, lanes(h ^ k, width)] = grads[k][...]
    mixed[...] = dot(full[...], weight_ref[...], (1, 1)).astype(BF16)
    for m in range(A):
        head = lanes(a ^ m, DH)
        outs[m][:, :DH] = q_ref[:, head]
        outs[m][:, DH : 2 * DH] = mixed[:, head]
        outs[m][:, 2 * DH :] = cot_piece(full, A, B, H, a ^ m, h)


def pack_body(A, *refs):
    for m in range(1, A):
        refs[-1][m - 1] = refs[A - 1 - m][...]


def collect_body(*refs):
    for m, ref in enumerate(refs[:-1]):
        refs[-1][m] = ref[:, 2 * DH :]


def join_body(*refs):
    for i, ref in enumerate(refs[:-1]):
        refs[-1][i] = ref[...]


def stage_body(*refs):
    half = len(refs) // 2
    for source, target in zip(refs[:half], refs[half:]):
        target[...] = source[...]


def forward_body(A, B, R, score_scale, owner_ref, block_ref, *refs):
    pair = B == 2
    piece_refs, own_refs, others, refs = refs[:A][::-1], refs[A : 2 * A], refs[2 * A : -4], refs[-4:]
    attn_ref, kvcat, weights_ref, kv = refs
    SEG = piece_refs[0].shape[0]
    parts = SEG // BLOCK
    count = 2 * SEG + R * BLOCK
    seg = lax.axis_index("seg")
    a, b = seg % A, seg // A
    if pair:
        for m in range(A):
            for part in range(parts):
                rows = slice(part * BLOCK, (part + 1) * BLOCK)
                kv[m * parts + part] = own_refs[m][rows, :]
                kv[(A + m) * parts + part] = others[1][m - 1, rows, :] if m else others[0][rows, :]
    else:
        kv = others[0]

    def place(other_a, other_b):
        slot = (other_b ^ b) * A + (other_a ^ a) if pair else other_b * A + (other_a ^ a)
        return slot * parts

    for m in range(A):
        seg_a = a ^ m
        s = b * A + seg_a
        prev_a = jnp.where(seg_a == 0, A - 1, seg_a - 1)
        prev_b = jnp.where(seg_a == 0, (b + B - 1) % B, b)
        far = count - SEG
        column = lax.broadcasted_iota(jnp.int32, (1, far), 1)
        hidden = (column < SEG) & (s == 0)
        for part in range(parts):
            at = part * BLOCK
            kvcat[m, at : at + BLOCK] = kv[place(seg_a, b) + part]
            kvcat[m, SEG + at : SEG + at + BLOCK] = kv[place(prev_a, prev_b) + part]
        for j in range(R):
            at = SEG + j * BLOCK
            owner, block = owner_ref[s, j], block_ref[s, j]
            kvcat[m, SEG + at : SEG + at + BLOCK] = kv[place(owner % A, owner // A) + jnp.maximum(block, 0)]
            hidden |= (column >= at) & (column < at + BLOCK) & (block < 0)
        bias = jnp.where(hidden, HIDDEN, 0.0)
        q = piece_refs[m][:, :DH]
        row = lax.broadcasted_iota(jnp.int32, (SEG, SEG), 0)
        col = lax.broadcasted_iota(jnp.int32, (SEG, SEG), 1)
        scale = score_scale * math.log2(math.e)
        near = jnp.where(row >= col, dot(q, kvcat[m, :SEG, :DH], (1, 1)) * scale, HIDDEN)
        rest = dot(q, kvcat[m, SEG:, :DH], (1, 1)) * scale + bias
        top = jnp.maximum(jnp.max(near, -1, keepdims=True), jnp.max(rest, -1, keepdims=True))
        near, rest = jnp.exp2(near - top), jnp.exp2(rest - top)
        inverse = 1.0 / (jnp.sum(near, -1, keepdims=True) + jnp.sum(rest, -1, keepdims=True))
        near, rest = near * inverse, rest * inverse
        weights_ref[m, :, :SEG] = near.astype(weights_ref.dtype)
        weights_ref[m, :, SEG:] = rest.astype(weights_ref.dtype)
        near, rest = near.astype(BF16), rest.astype(BF16)
        attn_ref[m] = (dot(near, kvcat[m, :SEG, DH:], (1, 0)) + dot(rest, kvcat[m, SEG:, DH:], (1, 0))).astype(BF16)


def backward_body(A, B, score_scale, attn_ref, kvcat, weights_ref, *refs):
    piece_refs, (dq_ref, own_ref, cache_ref, carry_ref) = refs[:A], refs[A:]
    SEG = piece_refs[0].shape[0]
    a = lax.axis_index("seg") % A
    for m in range(A):
        seg_a = a ^ m
        prev_a = jnp.where(seg_a == 0, A - 1, seg_a - 1)
        q, da = piece_refs[m][:, :DH], piece_refs[m][:, DH : 2 * DH]
        row_delta = jnp.sum(da.astype(F32) * attn_ref[m].astype(F32), -1, keepdims=True)
        weights = weights_ref[m]
        rounded = weights.astype(BF16)
        slopes = (weights.astype(F32) * (dot(da, kvcat[m, :, DH:], (1, 1)) - row_delta)).astype(BF16)
        dq_ref[m] = (score_scale * dot(slopes, kvcat[m, :, :DH], (1, 0))).astype(BF16)
        dk = score_scale * dot(slopes[:, : 2 * SEG], q, (0, 0))
        dv = dot(rounded[:, : 2 * SEG], da, (0, 0))
        own_ref[m, :, :DH] = dk[:SEG]
        own_ref[m, :, DH:] = dv[:SEG]
        dk, dv = dk[SEG:].astype(BF16), dv[SEG:].astype(BF16)
        cache_ref[prev_a ^ a, :, :DH] = dk
        cache_ref[prev_a ^ a, :, DH:] = dv

        @pl.when(seg_a == 0)
        def _():
            carry_ref[:, :DH] = dk
            carry_ref[:, DH:] = dv


def project_body(A, B, H, *refs):
    attns, gs, weight_ref, refs = refs[:A][::-1], refs[A : A + 2], refs[A + 2], refs[A + 4 :]
    keep_ref, pass_ref, send_ref, *proj_refs = refs[:-3]
    own, mixed, cots = refs[-3:]
    seg = lax.axis_index("seg")
    a, b = seg % A, seg // A
    h = lax.axis_index("head")
    SEG = attns[0].shape[1]
    for m in range(A):
        head = lanes(a ^ m, DH)
        own[:, head] = attns[m][m]
        for i in range(A):
            mixed[(m ^ i) * SEG : (m ^ i) * SEG + SEG, head] = attns[m][i]
    width = keep_ref.shape[1]
    keep_ref[...] = dot(own[...], weight_ref[:, lanes(h, width)], (1, 0))
    pass_ref[...] = dot(own[...], weight_ref[:, lanes(h ^ 2, width)], (1, 0))
    for k in (1, 3):
        at = k // 2 * width
        send_ref[:, at : at + width] = dot(own[...], weight_ref[:, lanes(h ^ k, width)], (1, 0)).astype(BF16)
    piece = gs[0].shape[3]
    for k in range(H):
        for m in range(A):
            cots[m * SEG : (m + 1) * SEG, lanes(h ^ k, piece)] = gs[k % 2][k // 2, m]
    if B == 2:
        rows = piece * H // 2
        proj_refs[0][...] = dot(cots[:, lanes(b, rows)], mixed[...], (0, 0))
        proj_refs[1][...] = dot(cots[:, lanes(1 - b, rows)], mixed[...], (0, 0)).astype(BF16)
    else:
        proj_refs[0][...] = dot(cots[...], mixed[...], (0, 0))


def merge_body(A, dq_ref, own_ref, cache_ref, carry_ref, *outs):
    a = lax.axis_index("seg") % A
    for m in range(A):
        outs[m][:, :DH] = dq_ref[m]
        late = jnp.where(a ^ m == A - 1, carry_ref[...], cache_ref[m])
        outs[m][:, DH:] = (own_ref[m] + late.astype(F32)).astype(BF16)


def place_body(A, B, *refs):
    pieces, projs, outs = refs[:A][::-1], refs[A:-4], refs[-4:]
    a = lax.axis_index("seg") % A
    for m in range(A):
        for i in range(3):
            outs[i][:, lanes(a ^ m, DH)] = pieces[m][:, i * DH : (i + 1) * DH]
    outs[3][...] = sum(term[...].astype(F32) for term in projs)


def per_device(queries, keys, values, out_grad, out_weight, retr_owner, retr_block):
    n, H = lax.axis_size("seg"), lax.axis_size("head")
    SEG, width = queries.shape
    A = width // DH
    B = n // A
    R = retr_owner.shape[1]
    D = out_weight.shape[1]
    score_scale = 1.0 / math.sqrt(DH)

    def over_a(x, m):
        return lax.ppermute(x, "seg", [(i, i // A * A + (i % A ^ m)) for i in range(n)])

    def over_b(x):
        return lax.ppermute(x, "seg", [(i, (i + A) % n) for i in range(n)])

    def back_b(x):
        return lax.ppermute(x, "seg", [(i, i - A) for i in range(A, n)])

    def over_head(x, k):
        return lax.ppermute(x, "head", [(i, i ^ k) for i in range(H)])

    def exchange(pieces):
        moved = {m: over_a(pieces[m], m) for m in reversed(range(1, A))}
        return [pieces[0]] + [moved[m] for m in range(1, A)]

    grads = [out_grad, over_head(out_grad, 1), over_head(out_grad, 2)]
    grads += [over_head(grads[2], 1)]

    cut = functools.partial(cut_body, A, B)
    kvs = exchange(call(cut, [shape((SEG, 2 * DH), BF16)] * A, [keys, values]))
    staged = call(stage_body, [shape(x.shape, BF16) for x in (out_weight, queries, out_grad)], [out_weight, queries, out_grad])
    early = [over_b(kvs[0])] if B == 2 else []
    kv = call(
        functools.partial(pack_body, A),
        [shape((A - 1, SEG, 2 * DH), BF16)],
        [*kvs[:0:-1], *early, staged[0]],
        specs=[VMEM] * (A - 1) + [ANY] * (1 + len(early)),
    )[0]
    out_weight, queries, grads[0] = staged
    if B == 2:
        kv = [*early, over_b(kv)]
    else:
        groups = [[j * A + i for j in range(B)] for i in range(A)]
        kv = lax.all_gather(jnp.concatenate([kvs[0][None], kv]), "seg", axis_index_groups=groups)
        kv = [kv.reshape(B * A * (SEG // BLOCK), BLOCK, 2 * DH)]
    sloped = call(
        functools.partial(slope_body, A, B, H),
        [shape((SEG, 2 * DH + width // H), BF16)] * A,
        [*grads, out_weight, queries],
        scratch=[pltpu.VMEM((SEG, D), BF16), pltpu.VMEM((SEG, width), BF16)],
        flops=2 * 10**8,
    )
    pieces = exchange(sloped)
    count = 2 * SEG + R * BLOCK
    cot = call(collect_body, [shape((A, SEG, width // H), BF16)], pieces)[0]
    far_cot = over_head(cot, 2)
    limit = 20 if B == 2 else 60
    attn, kvcat, weights = call(
        functools.partial(forward_body, A, B, R, score_scale),
        [shape((A, SEG, DH), BF16), shape((A, count, 2 * DH), BF16), shape((A, SEG, count), F32)],
        [retr_owner, retr_block, *pieces[::-1], *kvs, *kv],
        specs=[SMEM] * 2 + [VMEM] * (2 * A + len(kv)),
        scratch=[pltpu.VMEM((2 * A * (SEG // BLOCK), BLOCK, 2 * DH), BF16)],
        limit=limit,
        flops=10**11,
    )
    dq, own, cache, carry = call(
        functools.partial(backward_body, A, B, score_scale),
        [
            shape((A, SEG, DH), BF16),
            shape((A, SEG, 2 * DH), F32),
            shape((A, SEG, 2 * DH), BF16),
            shape((SEG, 2 * DH), BF16),
        ],
        [attn, kvcat, weights, *pieces],
        limit=limit,
        flops=10**11,
    )
    attns = exchange([attn] * A)
    carried = back_b(carry)
    cots = call(join_body, [shape((2, *cot.shape), BF16)], [cot, far_cot])[0]
    gs = [cots, over_head(cots, 1)]
    merged = call(
        functools.partial(merge_body, A), [shape((SEG, 3 * DH), BF16)] * A, [dq, own, cache, carried]
    )
    partials = [shape((SEG, D // H), F32)] * 2 + [shape((SEG, D // 2), BF16)]
    rows = D // A
    if B == 2:
        projs = [shape((rows // 2, width), F32), shape((rows // 2, width), BF16)]
    else:
        projs = [shape((rows, width), F32)]
    keep, passed, send, *proj = call(
        functools.partial(project_body, A, B, H),
        partials + projs,
        [*attns[::-1], *gs, out_weight, merged[0]],
        specs=[VMEM] * (A + 3) + [ANY],
        scratch=[
            pltpu.VMEM((SEG, width), BF16),
            pltpu.VMEM((A * SEG, width), BF16),
            pltpu.VMEM((A * SEG, rows), BF16),
        ],
    )
    moved = exchange(merged)
    block = D // H
    received = over_head(send, 1)
    passed = (passed + received[:, block:].astype(F32)).astype(BF16)
    if B == 2:
        proj = [proj[0], over_b(proj[1])]
    else:
        proj = [lax.psum_scatter(proj[0], "seg", scatter_dimension=0, axis_index_groups=groups, tiled=True)]
    *placed, proj_grad_t = call(
        functools.partial(place_body, A, B),
        [shape((SEG, width), BF16)] * 3 + [shape(proj[0].shape, F32)],
        [*moved[::-1], *proj],
        flops=10**11,
    )
    placed[0], keep = lax.optimization_barrier((placed[0], keep))
    layer_out = keep + received[:, :block].astype(F32) + over_head(passed, 2).astype(F32)
    return (layer_out.astype(BF16), *placed, proj_grad_t)


def solution(mesh):
    both = P("seg", "head")
    return jax.shard_map(
        per_device,
        mesh=mesh,
        in_specs=(both, both, both, both, P("head", None), P(), P()),
        out_specs=(both,) * 5,
        check_vma=False,
    )
```

```python
import functools
import math

import jax
import jax.numpy as jnp
from jax import lax
from jax.experimental import pallas as pl
from jax.experimental.pallas import tpu as pltpu
from jax.sharding import PartitionSpec as P

DH = 128
BLOCK = 128
F32 = jnp.float32
BF16 = jnp.bfloat16
HIDDEN = -1e30
TURN = (2, 3, 1, 0)
VMEM = pl.BlockSpec(memory_space=pltpu.VMEM)
ANY = pl.BlockSpec(memory_space=pl.ANY)
HBM = pl.BlockSpec(memory_space=pltpu.HBM)
SMEM = pl.BlockSpec(memory_space=pltpu.SMEM)


def dot(left, right, dims):
    return lax.dot_general(left, right, ((dims[:1], dims[1:]), ((), ())), preferred_element_type=F32)


def lanes(block, width):
    return pl.ds(pl.multiple_of(block * width, width), width)


def turned(pieces):
    return [pieces[m] for m in TURN]


def straight(refs):
    return [refs[TURN.index(m)] for m in range(len(TURN))]


def call(body, outs, operands, specs=None, scratch=(), limit=20, flops=1):
    return list(pl.pallas_call(
        body,
        out_shape=outs,
        in_specs=specs or [VMEM] * len(operands),
        out_specs=[VMEM] * len(outs),
        scratch_shapes=list(scratch),
        compiler_params=pltpu.CompilerParams(vmem_limit_bytes=limit * 2**20),
        cost_estimate=pl.CostEstimate(flops=flops, bytes_accessed=1, transcendentals=0),
    )(*operands))


def shape(dims, dtype):
    return jax.ShapeDtypeStruct(dims, dtype)


def cut_body(A, B, k_ref, v_ref, *outs):
    a = lax.axis_index("seg") % A
    for m in range(A):
        head = lanes(a ^ m, DH)
        outs[m][:, :DH] = k_ref[:, head]
        outs[m][:, DH:] = v_ref[:, head]


def cot_piece(full, A, B, H, other, h):
    total = full.shape[1]
    part, own = total // (A * H), total // (A * B)
    if own % part == 0:
        split = own // part
        return full[:, lanes(((h // split) * A + other) * split + h % split, part)]
    row = lax.broadcasted_iota(jnp.int32, (part * A, part), 0)
    col = lax.broadcasted_iota(jnp.int32, (part * A, part), 1)
    pick = (row == (col // own * A + other) * own + col % own).astype(BF16)
    return dot(full[:, lanes(h, part * A)], pick, (1, 0)).astype(BF16)


def slope_body(A, B, H, *refs):
    grads, weight_ref, q_ref, refs = refs[:2], refs[2], refs[3], refs[4:]
    outs, full, mixed = refs[:A], refs[-2], refs[-1]
    a = lax.axis_index("seg") % A
    h = lax.axis_index("head")
    width = grads[0].shape[2]
    for k in range(H):
        full[:, lanes(h ^ k, width)] = grads[k % 2][k // 2]
    mixed[...] = dot(full[...], weight_ref[...], (1, 1)).astype(BF16)
    for m in range(A):
        head = lanes(a ^ m, DH)
        outs[m][:, :DH] = q_ref[:, head]
        outs[m][:, DH : 2 * DH] = mixed[:, head]
        outs[m][:, 2 * DH :] = cot_piece(full, A, B, H, a ^ m, h)


def pack_body(A, *refs):
    for m in range(1, A):
        refs[-1][m - 1] = refs[TURN.index(m)][...]


def collect_body(*refs):
    for m, ref in enumerate(refs[:-1]):
        refs[-1][m] = ref[:, 2 * DH :]


def join_body(*refs):
    for i, ref in enumerate(refs[:-1]):
        refs[-1][i] = ref[...]


def stage_body(*refs):
    half = len(refs) // 2
    for source, target in zip(refs[:half], refs[half:]):
        target[...] = source[...]


def forward_body(A, B, R, score_scale, owner_ref, block_ref, *refs):
    pair = B == 2
    piece_refs, own_refs, others, refs = straight(refs[:A]), refs[A : 2 * A], refs[2 * A : -4], refs[-4:]
    attn_ref, kvcat, weights_ref, kv = refs
    SEG = piece_refs[0].shape[0]
    parts = SEG // BLOCK
    count = 2 * SEG + R * BLOCK
    seg = lax.axis_index("seg")
    a, b = seg % A, seg // A
    if pair:
        for m in range(A):
            for part in range(parts):
                rows = slice(part * BLOCK, (part + 1) * BLOCK)
                kv[m * parts + part] = own_refs[m][rows, :]
                kv[(A + m) * parts + part] = others[1][m - 1, rows, :] if m else others[0][rows, :]
    else:
        kv = others[0]

    def place(other_a, other_b):
        slot = (other_b ^ b) * A + (other_a ^ a) if pair else other_b * A + (other_a ^ a)
        return slot * parts

    for m in range(A):
        seg_a = a ^ m
        s = b * A + seg_a
        prev_a = jnp.where(seg_a == 0, A - 1, seg_a - 1)
        prev_b = jnp.where(seg_a == 0, (b + B - 1) % B, b)
        far = count - SEG
        column = lax.broadcasted_iota(jnp.int32, (1, far), 1)
        hidden = (column < SEG) & (s == 0)
        for part in range(parts):
            at = part * BLOCK
            kvcat[m, at : at + BLOCK] = kv[place(seg_a, b) + part]
            kvcat[m, SEG + at : SEG + at + BLOCK] = kv[place(prev_a, prev_b) + part]
        for j in range(R):
            at = SEG + j * BLOCK
            owner, block = owner_ref[s, j], block_ref[s, j]
            kvcat[m, SEG + at : SEG + at + BLOCK] = kv[place(owner % A, owner // A) + jnp.maximum(block, 0)]
            hidden |= (column >= at) & (column < at + BLOCK) & (block < 0)
        bias = jnp.where(hidden, HIDDEN, 0.0)
        q = piece_refs[m][:, :DH]
        row = lax.broadcasted_iota(jnp.int32, (SEG, SEG), 0)
        col = lax.broadcasted_iota(jnp.int32, (SEG, SEG), 1)
        scale = score_scale * math.log2(math.e)
        near = jnp.where(row >= col, dot(q, kvcat[m, :SEG, :DH], (1, 1)) * scale, HIDDEN)
        rest = dot(q, kvcat[m, SEG:, :DH], (1, 1)) * scale + bias
        top = jnp.maximum(jnp.max(near, -1, keepdims=True), jnp.max(rest, -1, keepdims=True))
        near, rest = jnp.exp2(near - top), jnp.exp2(rest - top)
        inverse = 1.0 / (jnp.sum(near, -1, keepdims=True) + jnp.sum(rest, -1, keepdims=True))
        near, rest = near * inverse, rest * inverse
        weights_ref[m, :, :SEG] = near.astype(weights_ref.dtype)
        weights_ref[m, :, SEG:] = rest.astype(weights_ref.dtype)
        near, rest = near.astype(BF16), rest.astype(BF16)
        attn_ref[m] = (dot(near, kvcat[m, :SEG, DH:], (1, 0)) + dot(rest, kvcat[m, SEG:, DH:], (1, 0))).astype(BF16)


def backward_body(A, B, score_scale, attn_ref, kvcat, weights_ref, *refs):
    piece_refs, (dq_ref, own_ref, cache_ref, carry_ref) = refs[:A], refs[A:]
    SEG = piece_refs[0].shape[0]
    a = lax.axis_index("seg") % A
    for m in range(A):
        seg_a = a ^ m
        prev_a = jnp.where(seg_a == 0, A - 1, seg_a - 1)
        q, da = piece_refs[m][:, :DH], piece_refs[m][:, DH : 2 * DH]
        row_delta = jnp.sum(da.astype(F32) * attn_ref[m].astype(F32), -1, keepdims=True)
        weights = weights_ref[m]
        rounded = weights.astype(BF16)
        slopes = (weights.astype(F32) * (dot(da, kvcat[m, :, DH:], (1, 1)) - row_delta)).astype(BF16)
        dq_ref[m] = (score_scale * dot(slopes, kvcat[m, :, :DH], (1, 0))).astype(BF16)
        dk = score_scale * dot(slopes[:, : 2 * SEG], q, (0, 0))
        dv = dot(rounded[:, : 2 * SEG], da, (0, 0))
        own_ref[m, :, :DH] = dk[:SEG]
        own_ref[m, :, DH:] = dv[:SEG]
        dk, dv = dk[SEG:].astype(BF16), dv[SEG:].astype(BF16)
        cache_ref[prev_a ^ a, :, :DH] = dk
        cache_ref[prev_a ^ a, :, DH:] = dv

        @pl.when(seg_a == 0)
        def _():
            carry_ref[:, :DH] = dk
            carry_ref[:, DH:] = dv


def project_body(A, B, H, *refs):
    attns, gs, weight_ref, refs = straight(refs[:A]), refs[A : A + 2], refs[A + 2], refs[A + 3 :]
    keep_ref, pass_ref, send_ref, *proj_refs = refs[:-3]
    own, mixed, cots = refs[-3:]
    seg = lax.axis_index("seg")
    a, b = seg % A, seg // A
    h = lax.axis_index("head")
    SEG = attns[0].shape[1]
    for m in range(A):
        head = lanes(a ^ m, DH)
        own[:, head] = attns[m][m]
        for i in range(A):
            mixed[(m ^ i) * SEG : (m ^ i) * SEG + SEG, head] = attns[m][i]
    width = keep_ref.shape[1]
    keep_ref[...] = dot(own[...], weight_ref[:, lanes(h, width)], (1, 0))
    pass_ref[...] = dot(own[...], weight_ref[:, lanes(h ^ 2, width)], (1, 0))
    for k in (1, 3):
        at = k // 2 * width
        send_ref[:, at : at + width] = dot(own[...], weight_ref[:, lanes(h ^ k, width)], (1, 0)).astype(BF16)
    piece = gs[0].shape[3]
    for k in range(H):
        for m in range(A):
            cots[m * SEG : (m + 1) * SEG, lanes(h ^ k, piece)] = gs[k % 2][k // 2, m]
    if B == 2:
        rows = piece * H // 2
        proj_refs[0][...] = dot(cots[:, lanes(b, rows)], mixed[...], (0, 0))
        proj_refs[1][...] = dot(cots[:, lanes(1 - b, rows)], mixed[...], (0, 0)).astype(BF16)
    else:
        proj_refs[0][...] = dot(cots[...], mixed[...], (0, 0))


def merge_body(A, dq_ref, own_ref, cache_ref, carry_ref, *outs):
    a = lax.axis_index("seg") % A
    for m in range(A):
        outs[m][:, :DH] = dq_ref[m]
        late = jnp.where(a ^ m == A - 1, carry_ref[...], cache_ref[m])
        outs[m][:, DH:] = (own_ref[m] + late.astype(F32)).astype(BF16)


def token_body(*refs):
    refs[-1][...] = jnp.zeros_like(refs[-1])


def place_body(A, B, *refs):
    pieces, terms, projs, outs = straight(refs[:A]), refs[A : A + 3], refs[A + 3 : -6], refs[-5:]
    a = lax.axis_index("seg") % A
    for m in range(A):
        for i in range(3):
            outs[1 + i][:, lanes(a ^ m, DH)] = pieces[m][:, i * DH : (i + 1) * DH]
    outs[0][...] = sum(term[...].astype(F32) for term in terms).astype(BF16)
    outs[4][...] = sum(term[...].astype(F32) for term in projs)


def per_device(queries, keys, values, out_grad, out_weight, retr_owner, retr_block):
    n, H = lax.axis_size("seg"), lax.axis_size("head")
    SEG, width = queries.shape
    A = width // DH
    B = n // A
    R = retr_owner.shape[1]
    D = out_weight.shape[1]
    score_scale = 1.0 / math.sqrt(DH)

    def over_a(x, m):
        return lax.ppermute(x, "seg", [(i, i // A * A + (i % A ^ m)) for i in range(n)])

    def over_b(x):
        return lax.ppermute(x, "seg", [(i, (i + A) % n) for i in range(n)])

    def back_b(x):
        return lax.ppermute(x, "seg", [(i, i - A) for i in range(A, n)])

    def over_head(x, k):
        return lax.ppermute(x, "head", [(i, i ^ k) for i in range(H)])

    def exchange(pieces):
        moved = {m: over_a(pieces[m], m) for m in reversed(range(1, A))}
        return [pieces[0]] + [moved[m] for m in range(1, A)]


    cut = functools.partial(cut_body, A, B)
    kvs = call(cut, [shape((SEG, 2 * DH), BF16)] * A, [keys, values])
    out_grad, kvs[0] = lax.optimization_barrier((out_grad, kvs[0]))
    far_grad = over_head(out_grad, 2)
    kvs = exchange(kvs)
    staged = call(stage_body, [shape(x.shape, BF16) for x in (out_weight, queries, out_grad)], [out_weight, queries, out_grad])
    early = [over_b(kvs[0])] if B == 2 else []
    kv = call(
        functools.partial(pack_body, A),
        [shape((A - 1, SEG, 2 * DH), BF16)],
        [*turned(kvs)[:-1], *early, staged[0]],
        specs=[VMEM] * (A - 1) + [ANY] * (1 + len(early)),
        flops=40 * 10**8,
    )[0]
    out_weight, queries, near_grad = staged
    both = call(join_body, [shape((2, SEG, width), BF16)], [near_grad, far_grad])[0]
    grads = [both, over_head(both, 1)]
    if B == 2:
        kv = [*early, over_b(kv)]
    else:
        groups = [[j * A + i for j in range(B)] for i in range(A)]
        kv = lax.all_gather(jnp.concatenate([kvs[0][None], kv]), "seg", axis_index_groups=groups)
        kv = [kv.reshape(B * A * (SEG // BLOCK), BLOCK, 2 * DH)]
    sloped = call(
        functools.partial(slope_body, A, B, H),
        [shape((SEG, 2 * DH + width // H), BF16)] * A,
        [*grads, out_weight, queries],
        scratch=[pltpu.VMEM((SEG, D), BF16), pltpu.VMEM((SEG, width), BF16)],
        flops=1,
    )
    pieces = exchange(sloped)
    count = 2 * SEG + R * BLOCK
    cot = call(collect_body, [shape((A, SEG, width // H), BF16)], pieces)[0]
    far_cot = over_head(cot, 2)
    limit = 20 if B == 2 else 60
    attn, kvcat, weights = call(
        functools.partial(forward_body, A, B, R, score_scale),
        [shape((A, SEG, DH), BF16), shape((A, count, 2 * DH), BF16), shape((A, SEG, count), F32)],
        [retr_owner, retr_block, *turned(pieces), *kvs, *kv],
        specs=[SMEM] * 2 + [VMEM] * (2 * A + len(kv)),
        scratch=[pltpu.VMEM((2 * A * (SEG // BLOCK), BLOCK, 2 * DH), BF16)],
        limit=limit,
        flops=10**11,
    )
    dq, own, cache, carry = call(
        functools.partial(backward_body, A, B, score_scale),
        [
            shape((A, SEG, DH), BF16),
            shape((A, SEG, 2 * DH), F32),
            shape((A, SEG, 2 * DH), BF16),
            shape((SEG, 2 * DH), BF16),
        ],
        [attn, kvcat, weights, *pieces],
        limit=limit,
        flops=10**11,
    )
    attns = exchange([attn] * A)
    carried = back_b(carry)
    cots = call(join_body, [shape((2, *cot.shape), BF16)], [cot, far_cot])[0]
    gs = [cots, over_head(cots, 1)]
    merged = call(
        functools.partial(merge_body, A),
        [shape((SEG, 3 * DH), BF16)] * A,
        [dq, own, cache, carried],
        flops=10 * 10**9,
    )
    partials = [shape((SEG, D // H), F32)] * 2 + [shape((SEG, D // 2), BF16)]
    rows = D // A
    if B == 2:
        projs = [shape((rows // 2, width), F32), shape((rows // 2, width), BF16)]
    else:
        projs = [shape((rows, width), F32)]
    keep, passed, send, *proj = call(
        functools.partial(project_body, A, B, H),
        partials + projs,
        [*turned(attns), *gs, out_weight],
        specs=[VMEM] * (A + 3),
        scratch=[
            pltpu.VMEM((SEG, width), BF16),
            pltpu.VMEM((A * SEG, width), BF16),
            pltpu.VMEM((A * SEG, rows), BF16),
        ],
    )
    moved = exchange(merged)
    block = D // H
    received = over_head(send, 1)
    passed = (passed + received[:, block:].astype(F32)).astype(BF16)
    if B == 2:
        proj = [proj[0], over_b(proj[1])]
    else:
        proj = [lax.psum_scatter(proj[0], "seg", scatter_dimension=0, axis_index_groups=groups, tiled=True)]
    token = call(token_body, [shape((8, 128), F32)], [*moved[1:], *proj[1:]], specs=[ANY] * (A - 2 + len(proj)), flops=10**11)
    return tuple(
        call(
            functools.partial(place_body, A, B),
            [shape((SEG, width), BF16)] * 4 + [shape(proj[0].shape, F32)],
            [*turned(moved), keep, received[:, :block], over_head(passed, 2), *proj, *token],
            specs=[VMEM] * (A + 3 + len(proj)) + [ANY],
        )
    )


def solution(mesh):
    both = P("seg", "head")
    return jax.shard_map(
        per_device,
        mesh=mesh,
        in_specs=(both, both, both, both, P("head", None), P(), P()),
        out_specs=(both,) * 5,
        check_vma=False,
    )
```

```python
import functools
import math

import jax
import jax.numpy as jnp
from jax import lax
from jax.experimental import pallas as pl
from jax.experimental.pallas import tpu as pltpu
from jax.sharding import PartitionSpec as P

DH = 128
BLOCK = 128
F32 = jnp.float32
BF16 = jnp.bfloat16
HIDDEN = -1e30
TURN = (2, 3, 1, 0)
LAST = (3, 2, 1, 0)
VMEM = pl.BlockSpec(memory_space=pltpu.VMEM)
ANY = pl.BlockSpec(memory_space=pl.ANY)
HBM = pl.BlockSpec(memory_space=pltpu.HBM)
SMEM = pl.BlockSpec(memory_space=pltpu.SMEM)


def dot(left, right, dims):
    return lax.dot_general(left, right, ((dims[:1], dims[1:]), ((), ())), preferred_element_type=F32)


def lanes(block, width):
    return pl.ds(pl.multiple_of(block * width, width), width)


def turned(pieces, turn=TURN):
    return [pieces[m] for m in turn]


def straight(refs, turn=TURN):
    return [refs[turn.index(m)] for m in range(len(turn))]


def call(body, outs, operands, specs=None, scratch=(), limit=20, flops=1):
    return list(pl.pallas_call(
        body,
        out_shape=outs,
        in_specs=specs or [VMEM] * len(operands),
        out_specs=[VMEM] * len(outs),
        scratch_shapes=list(scratch),
        compiler_params=pltpu.CompilerParams(vmem_limit_bytes=limit * 2**20),
        cost_estimate=pl.CostEstimate(flops=flops, bytes_accessed=1, transcendentals=0),
    )(*operands))


def shape(dims, dtype):
    return jax.ShapeDtypeStruct(dims, dtype)


def cut_body(A, B, k_ref, v_ref, *outs):
    a = lax.axis_index("seg") % A
    for m in range(A):
        head = lanes(a ^ m, DH)
        outs[m][:, :DH] = k_ref[:, head]
        outs[m][:, DH:] = v_ref[:, head]


def cot_piece(full, A, B, H, other, h):
    total = full.shape[1]
    part, own = total // (A * H), total // (A * B)
    if own % part == 0:
        split = own // part
        return full[:, lanes(((h // split) * A + other) * split + h % split, part)]
    row = lax.broadcasted_iota(jnp.int32, (part * A, part), 0)
    col = lax.broadcasted_iota(jnp.int32, (part * A, part), 1)
    pick = (row == (col // own * A + other) * own + col % own).astype(BF16)
    return dot(full[:, lanes(h, part * A)], pick, (1, 0)).astype(BF16)


def slope_body(A, B, H, *refs):
    grads, weight_ref, q_ref, refs = refs[:2], refs[2], refs[3], refs[4:]
    outs, full, mixed = refs[:A], refs[-2], refs[-1]
    a = lax.axis_index("seg") % A
    h = lax.axis_index("head")
    width = grads[0].shape[2]
    for k in range(H):
        full[:, lanes(h ^ k, width)] = grads[k % 2][k // 2]
    mixed[...] = dot(full[...], weight_ref[...], (1, 1)).astype(BF16)
    for m in range(A):
        head = lanes(a ^ m, DH)
        outs[m][:, :DH] = q_ref[:, head]
        outs[m][:, DH : 2 * DH] = mixed[:, head]
        outs[m][:, 2 * DH :] = cot_piece(full, A, B, H, a ^ m, h)


def pack_body(A, *refs):
    for m in range(1, A):
        refs[-1][m - 1] = refs[TURN.index(m)][...]


def collect_body(*refs):
    for m, ref in enumerate(refs[:-1]):
        refs[-1][m] = ref[:, 2 * DH :]


def join_body(*refs):
    for i, ref in enumerate(refs[:-1]):
        refs[-1][i] = ref[...]


def stage_body(*refs):
    half = len(refs) // 2
    for source, target in zip(refs[:half], refs[half:]):
        target[...] = source[...]


def forward_body(A, B, R, score_scale, owner_ref, block_ref, *refs):
    pair = B == 2
    piece_refs, own_refs, others, refs = straight(refs[:A]), refs[A : 2 * A], refs[2 * A : -4], refs[-4:]
    attn_ref, kvcat, weights_ref, kv = refs
    SEG = piece_refs[0].shape[0]
    parts = SEG // BLOCK
    count = 2 * SEG + R * BLOCK
    seg = lax.axis_index("seg")
    a, b = seg % A, seg // A
    if pair:
        for m in range(A):
            for part in range(parts):
                rows = slice(part * BLOCK, (part + 1) * BLOCK)
                kv[m * parts + part] = own_refs[m][rows, :]
                kv[(A + m) * parts + part] = others[1][m - 1, rows, :] if m else others[0][rows, :]
    else:
        kv = others[0]

    def place(other_a, other_b):
        slot = (other_b ^ b) * A + (other_a ^ a) if pair else other_b * A + (other_a ^ a)
        return slot * parts

    row = lax.broadcasted_iota(jnp.int32, (SEG, SEG), 0)
    col = lax.broadcasted_iota(jnp.int32, (SEG, SEG), 1)
    scale = score_scale * math.log2(math.e)
    far = count - SEG
    column = lax.broadcasted_iota(jnp.int32, (1, far), 1)

    def score(m):
        seg_a = a ^ m
        s = b * A + seg_a
        prev_a = jnp.where(seg_a == 0, A - 1, seg_a - 1)
        prev_b = jnp.where(seg_a == 0, (b + B - 1) % B, b)
        hidden = (column < SEG) & (s == 0)
        for part in range(parts):
            at = part * BLOCK
            kvcat[m, at : at + BLOCK] = kv[place(seg_a, b) + part]
            kvcat[m, SEG + at : SEG + at + BLOCK] = kv[place(prev_a, prev_b) + part]
        for j in range(R):
            at = SEG + j * BLOCK
            owner, block = owner_ref[s, j], block_ref[s, j]
            kvcat[m, SEG + at : SEG + at + BLOCK] = kv[place(owner % A, owner // A) + jnp.maximum(block, 0)]
            hidden |= (column >= at) & (column < at + BLOCK) & (block < 0)
        q = piece_refs[m][:, :DH]
        near = jnp.where(row >= col, dot(q, kvcat[m, :SEG, :DH], (1, 1)) * scale, HIDDEN)
        return near, dot(q, kvcat[m, SEG:, :DH], (1, 1)) * scale + jnp.where(hidden, HIDDEN, 0.0)

    def mix(m, near, rest):
        top = jnp.maximum(jnp.max(near, -1, keepdims=True), jnp.max(rest, -1, keepdims=True))
        near, rest = jnp.exp2(near - top), jnp.exp2(rest - top)
        inverse = 1.0 / (jnp.sum(near, -1, keepdims=True) + jnp.sum(rest, -1, keepdims=True))
        near, rest = near * inverse, rest * inverse
        weights_ref[m, :, :SEG] = near
        weights_ref[m, :, SEG:] = rest
        near, rest = near.astype(BF16), rest.astype(BF16)
        attn_ref[m] = (dot(near, kvcat[m, :SEG, DH:], (1, 0)) + dot(rest, kvcat[m, SEG:, DH:], (1, 0))).astype(BF16)

    scores = score(0)
    for m in range(A):
        later = score(m + 1) if m + 1 < A else None
        mix(m, *scores)
        scores = later


def backward_body(A, B, score_scale, attn_ref, kvcat, weights_ref, *refs):
    piece_refs, (dq_ref, own_ref, cache_ref, carry_ref) = refs[:A], refs[A:]
    SEG = piece_refs[0].shape[0]
    a = lax.axis_index("seg") % A
    for m in range(A):
        seg_a = a ^ m
        prev_a = jnp.where(seg_a == 0, A - 1, seg_a - 1)
        q, da = piece_refs[m][:, :DH], piece_refs[m][:, DH : 2 * DH]
        row_delta = jnp.sum(da.astype(F32) * attn_ref[m].astype(F32), -1, keepdims=True)
        weights = weights_ref[m]
        rounded = weights.astype(BF16)
        slopes = (weights.astype(F32) * (dot(da, kvcat[m, :, DH:], (1, 1)) - row_delta)).astype(BF16)
        dq_ref[m] = (score_scale * dot(slopes, kvcat[m, :, :DH], (1, 0))).astype(BF16)
        dk = score_scale * dot(slopes[:, : 2 * SEG], q, (0, 0))
        dv = dot(rounded[:, : 2 * SEG], da, (0, 0))
        own_ref[m, :, :DH] = dk[:SEG]
        own_ref[m, :, DH:] = dv[:SEG]
        dk, dv = dk[SEG:].astype(BF16), dv[SEG:].astype(BF16)
        cache_ref[prev_a ^ a, :, :DH] = dk
        cache_ref[prev_a ^ a, :, DH:] = dv

        @pl.when(seg_a == 0)
        def _():
            carry_ref[:, :DH] = dk
            carry_ref[:, DH:] = dv


def project_body(A, B, H, *refs):
    attns, gs, weight_ref, refs = straight(refs[:A]), refs[A : A + 2], refs[A + 2], refs[A + 3 :]
    keep_ref, pass_ref, send_ref, *proj_refs = refs[:-3]
    own, mixed, cots = refs[-3:]
    seg = lax.axis_index("seg")
    a, b = seg % A, seg // A
    h = lax.axis_index("head")
    SEG = attns[0].shape[1]
    for m in range(A):
        head = lanes(a ^ m, DH)
        own[:, head] = attns[m][m]
        for i in range(A):
            mixed[(m ^ i) * SEG : (m ^ i) * SEG + SEG, head] = attns[m][i]
    width = keep_ref.shape[1]
    keep_ref[...] = dot(own[...], weight_ref[:, lanes(h, width)], (1, 0))
    pass_ref[...] = dot(own[...], weight_ref[:, lanes(h ^ 2, width)], (1, 0))
    for k in (1, 3):
        at = k // 2 * width
        send_ref[:, at : at + width] = dot(own[...], weight_ref[:, lanes(h ^ k, width)], (1, 0)).astype(BF16)
    piece = gs[0].shape[3]
    for k in range(H):
        for m in range(A):
            cots[m * SEG : (m + 1) * SEG, lanes(h ^ k, piece)] = gs[k % 2][k // 2, m]
    if B == 2:
        rows = piece * H // 2
        proj_refs[0][...] = dot(cots[:, lanes(b, rows)], mixed[...], (0, 0))
        proj_refs[1][...] = dot(cots[:, lanes(1 - b, rows)], mixed[...], (0, 0)).astype(BF16)
    else:
        proj_refs[0][...] = dot(cots[...], mixed[...], (0, 0))


def merge_body(A, dq_ref, own_ref, cache_ref, carry_ref, *outs):
    a = lax.axis_index("seg") % A
    for m in range(A):
        outs[m][:, :DH] = dq_ref[m]
        late = jnp.where(a ^ m == A - 1, carry_ref[...], cache_ref[m])
        outs[m][:, DH:] = (own_ref[m] + late.astype(F32)).astype(BF16)


def token_body(*refs):
    refs[-1][...] = jnp.zeros_like(refs[-1])


def place_body(A, B, *refs):
    pieces, terms, projs, outs = straight(refs[:A], LAST), refs[A : A + 3], refs[A + 3 : -6], refs[-5:]
    a = lax.axis_index("seg") % A
    for m in range(A):
        for i in range(3):
            outs[1 + i][:, lanes(a ^ m, DH)] = pieces[m][:, i * DH : (i + 1) * DH]
    outs[0][...] = sum(term[...].astype(F32) for term in terms).astype(BF16)
    outs[4][...] = sum(term[...].astype(F32) for term in projs)


def per_device(queries, keys, values, out_grad, out_weight, retr_owner, retr_block):
    n, H = lax.axis_size("seg"), lax.axis_size("head")
    SEG, width = queries.shape
    A = width // DH
    B = n // A
    R = retr_owner.shape[1]
    D = out_weight.shape[1]
    score_scale = 1.0 / math.sqrt(DH)

    def over_a(x, m):
        return lax.ppermute(x, "seg", [(i, i // A * A + (i % A ^ m)) for i in range(n)])

    def over_b(x):
        return lax.ppermute(x, "seg", [(i, (i + A) % n) for i in range(n)])

    def back_b(x):
        return lax.ppermute(x, "seg", [(i, i - A) for i in range(A, n)])

    def over_head(x, k):
        return lax.ppermute(x, "head", [(i, i ^ k) for i in range(H)])

    def exchange(pieces):
        moved = {m: over_a(pieces[m], m) for m in reversed(range(1, A))}
        return [pieces[0]] + [moved[m] for m in range(1, A)]


    cut = functools.partial(cut_body, A, B)
    kvs = call(cut, [shape((SEG, 2 * DH), BF16)] * A, [keys, values])
    out_grad, kvs[0] = lax.optimization_barrier((out_grad, kvs[0]))
    far_grad = over_head(out_grad, 2)
    kvs = exchange(kvs)
    staged = call(stage_body, [shape(x.shape, BF16) for x in (out_weight, queries, out_grad)], [out_weight, queries, out_grad])
    early = [over_b(kvs[0])] if B == 2 else []
    kv = call(
        functools.partial(pack_body, A),
        [shape((A - 1, SEG, 2 * DH), BF16)],
        [*turned(kvs)[:-1], *early, staged[0]],
        specs=[VMEM] * (A - 1) + [ANY] * (1 + len(early)),
        flops=40 * 10**8,
    )[0]
    out_weight, queries, near_grad = staged
    both = call(join_body, [shape((2, SEG, width), BF16)], [near_grad, far_grad])[0]
    grads = [both, over_head(both, 1)]
    if B == 2:
        kv = [*early, over_b(kv)]
    else:
        groups = [[j * A + i for j in range(B)] for i in range(A)]
        kv = lax.all_gather(jnp.concatenate([kvs[0][None], kv]), "seg", axis_index_groups=groups)
        kv = [kv.reshape(B * A * (SEG // BLOCK), BLOCK, 2 * DH)]
    sloped = call(
        functools.partial(slope_body, A, B, H),
        [shape((SEG, 2 * DH + width // H), BF16)] * A,
        [*grads, out_weight, queries],
        scratch=[pltpu.VMEM((SEG, D), BF16), pltpu.VMEM((SEG, width), BF16)],
        flops=1,
    )
    pieces = exchange(sloped)
    count = 2 * SEG + R * BLOCK
    cot = call(collect_body, [shape((A, SEG, width // H), BF16)], pieces)[0]
    far_cot = over_head(cot, 2)
    limit = 20 if B == 2 else 60
    attn, kvcat, weights = call(
        functools.partial(forward_body, A, B, R, score_scale),
        [shape((A, SEG, DH), BF16), shape((A, count, 2 * DH), BF16), shape((A, SEG, count), F32)],
        [retr_owner, retr_block, *turned(pieces), *kvs, *kv],
        specs=[SMEM] * 2 + [VMEM] * (2 * A + len(kv)),
        scratch=[pltpu.VMEM((2 * A * (SEG // BLOCK), BLOCK, 2 * DH), BF16)],
        limit=limit,
        flops=10**11,
    )
    dq, own, cache, carry = call(
        functools.partial(backward_body, A, B, score_scale),
        [
            shape((A, SEG, DH), BF16),
            shape((A, SEG, 2 * DH), F32),
            shape((A, SEG, 2 * DH), BF16),
            shape((SEG, 2 * DH), BF16),
        ],
        [attn, kvcat, weights, *pieces],
        limit=limit,
        flops=10**11,
    )
    attns = exchange([attn] * A)
    carried = back_b(carry)
    cots = call(join_body, [shape((2, *cot.shape), BF16)], [cot, far_cot])[0]
    gs = [cots, over_head(cots, 1)]
    merged = call(
        functools.partial(merge_body, A),
        [shape((SEG, 3 * DH), BF16)] * A,
        [dq, own, cache, carried],
        flops=10 * 10**9,
    )
    partials = [shape((SEG, D // H), F32)] * 2 + [shape((SEG, D // 2), BF16)]
    rows = D // A
    if B == 2:
        projs = [shape((rows // 2, width), F32), shape((rows // 2, width), BF16)]
    else:
        projs = [shape((rows, width), F32)]
    keep, passed, send, *proj = call(
        functools.partial(project_body, A, B, H),
        partials + projs,
        [*turned(attns), *gs, out_weight],
        specs=[VMEM] * (A + 3),
        scratch=[
            pltpu.VMEM((SEG, width), BF16),
            pltpu.VMEM((A * SEG, width), BF16),
            pltpu.VMEM((A * SEG, rows), BF16),
        ],
    )
    moved = exchange(merged)
    block = D // H
    received = over_head(send, 1)
    passed = (passed + received[:, block:].astype(F32)).astype(BF16)
    if B == 2:
        proj = [proj[0], over_b(proj[1])]
    else:
        proj = [lax.psum_scatter(proj[0], "seg", scatter_dimension=0, axis_index_groups=groups, tiled=True)]
    token = call(token_body, [shape((8, 128), F32)], [*moved[1:], *proj[1:]], specs=[ANY] * (A - 2 + len(proj)), flops=10**11)
    return tuple(
        call(
            functools.partial(place_body, A, B),
            [shape((SEG, width), BF16)] * 4 + [shape(proj[0].shape, F32)],
            [*turned(moved, LAST), keep, received[:, :block], over_head(passed, 2), *proj, *token],
            specs=[VMEM] * (A + 3 + len(proj)) + [ANY],
        )
    )


def solution(mesh):
    both = P("seg", "head")
    return jax.shard_map(
        per_device,
        mesh=mesh,
        in_specs=(both, both, both, both, P("head", None), P(), P()),
        out_specs=(both,) * 5,
        check_vma=False,
    )
```

```python
import functools
import math

import jax
import jax.numpy as jnp
from jax import lax
from jax.experimental import pallas as pl
from jax.experimental.pallas import tpu as pltpu
from jax.sharding import PartitionSpec as P

DH = 128
BLOCK = 128
F32 = jnp.float32
BF16 = jnp.bfloat16
HIDDEN = -1e30
TURN = (2, 3, 1, 0)
LAST = (3, 2, 1, 0)
VMEM = pl.BlockSpec(memory_space=pltpu.VMEM)
ANY = pl.BlockSpec(memory_space=pl.ANY)
HBM = pl.BlockSpec(memory_space=pltpu.HBM)
SMEM = pl.BlockSpec(memory_space=pltpu.SMEM)


def dot(left, right, dims):
    return lax.dot_general(left, right, ((dims[:1], dims[1:]), ((), ())), preferred_element_type=F32)


def lanes(block, width):
    return pl.ds(pl.multiple_of(block * width, width), width)


def turned(pieces, turn=TURN):
    return [pieces[m] for m in turn]


def straight(refs, turn=TURN):
    return [refs[turn.index(m)] for m in range(len(turn))]


def call(body, outs, operands, specs=None, scratch=(), limit=20, flops=1):
    return list(pl.pallas_call(
        body,
        out_shape=outs,
        in_specs=specs or [VMEM] * len(operands),
        out_specs=[VMEM] * len(outs),
        scratch_shapes=list(scratch),
        compiler_params=pltpu.CompilerParams(vmem_limit_bytes=limit * 2**20),
        cost_estimate=pl.CostEstimate(flops=flops, bytes_accessed=1, transcendentals=0),
    )(*operands))


def shape(dims, dtype):
    return jax.ShapeDtypeStruct(dims, dtype)


def cut_body(A, B, k_ref, v_ref, *outs):
    a = lax.axis_index("seg") % A
    for m in range(A):
        head = lanes(a ^ m, DH)
        outs[m][:, :DH] = k_ref[:, head]
        outs[m][:, DH:] = v_ref[:, head]


def cot_piece(full, A, B, H, other, h):
    total = full.shape[1]
    part, own = total // (A * H), total // (A * B)
    if own % part == 0:
        split = own // part
        return full[:, lanes(((h // split) * A + other) * split + h % split, part)]
    row = lax.broadcasted_iota(jnp.int32, (part * A, part), 0)
    col = lax.broadcasted_iota(jnp.int32, (part * A, part), 1)
    pick = (row == (col // own * A + other) * own + col % own).astype(BF16)
    return dot(full[:, lanes(h, part * A)], pick, (1, 0)).astype(BF16)


def slope_body(A, B, H, *refs):
    grads, weight_ref, q_ref, refs = refs[:2], refs[2], refs[3], refs[4:]
    outs, full, mixed = refs[:A], refs[-2], refs[-1]
    a = lax.axis_index("seg") % A
    h = lax.axis_index("head")
    width = grads[0].shape[2]
    for k in range(H):
        full[:, lanes(h ^ k, width)] = grads[k % 2][k // 2]
    mixed[...] = dot(full[...], weight_ref[...], (1, 1)).astype(BF16)
    for m in range(A):
        head = lanes(a ^ m, DH)
        outs[m][:, :DH] = q_ref[:, head]
        outs[m][:, DH : 2 * DH] = mixed[:, head]
        outs[m][:, 2 * DH :] = cot_piece(full, A, B, H, a ^ m, h)


def pack_body(A, *refs):
    for m in range(1, A):
        refs[-1][m - 1] = refs[TURN.index(m)][...]


def collect_body(*refs):
    for m, ref in enumerate(refs[:-1]):
        refs[-1][m] = ref[:, 2 * DH :]


def join_body(*refs):
    for i, ref in enumerate(refs[:-1]):
        refs[-1][i] = ref[...]


def stage_body(*refs):
    half = len(refs) // 2
    for source, target in zip(refs[:half], refs[half:]):
        target[...] = source[...]


def forward_body(A, B, R, score_scale, owner_ref, block_ref, *refs):
    pair = B == 2
    piece_refs, own_refs, others, refs = straight(refs[:A], LAST), refs[A : 2 * A], refs[2 * A : -4], refs[-4:]
    attn_ref, kvcat, weights_ref, kv = refs
    SEG = piece_refs[0].shape[0]
    parts = SEG // BLOCK
    count = 2 * SEG + R * BLOCK
    seg = lax.axis_index("seg")
    a, b = seg % A, seg // A
    if pair:
        for m in range(A):
            for part in range(parts):
                rows = slice(part * BLOCK, (part + 1) * BLOCK)
                kv[m * parts + part] = own_refs[m][rows, :]
                kv[(A + m) * parts + part] = others[1][m - 1, rows, :] if m else others[0][rows, :]
    else:
        kv = others[0]

    def place(other_a, other_b):
        slot = (other_b ^ b) * A + (other_a ^ a) if pair else other_b * A + (other_a ^ a)
        return slot * parts

    row = lax.broadcasted_iota(jnp.int32, (SEG, SEG), 0)
    col = lax.broadcasted_iota(jnp.int32, (SEG, SEG), 1)
    scale = score_scale * math.log2(math.e)
    far = count - SEG
    column = lax.broadcasted_iota(jnp.int32, (1, far), 1)

    def score(m):
        seg_a = a ^ m
        s = b * A + seg_a
        prev_a = jnp.where(seg_a == 0, A - 1, seg_a - 1)
        prev_b = jnp.where(seg_a == 0, (b + B - 1) % B, b)
        hidden = (column < SEG) & (s == 0)
        for part in range(parts):
            at = part * BLOCK
            kvcat[m, at : at + BLOCK] = kv[place(seg_a, b) + part]
            kvcat[m, SEG + at : SEG + at + BLOCK] = kv[place(prev_a, prev_b) + part]
        for j in range(R):
            at = SEG + j * BLOCK
            owner, block = owner_ref[s, j], block_ref[s, j]
            kvcat[m, SEG + at : SEG + at + BLOCK] = kv[place(owner % A, owner // A) + jnp.maximum(block, 0)]
            hidden |= (column >= at) & (column < at + BLOCK) & (block < 0)
        q = piece_refs[m][:, :DH]
        near = jnp.where(row >= col, dot(q, kvcat[m, :SEG, :DH], (1, 1)) * scale, HIDDEN)
        return near, dot(q, kvcat[m, SEG:, :DH], (1, 1)) * scale + jnp.where(hidden, HIDDEN, 0.0)

    def mix(m, near, rest):
        top = jnp.maximum(jnp.max(near, -1, keepdims=True), jnp.max(rest, -1, keepdims=True))
        near, rest = jnp.exp2(near - top), jnp.exp2(rest - top)
        inverse = 1.0 / (jnp.sum(near, -1, keepdims=True) + jnp.sum(rest, -1, keepdims=True))
        near, rest = near * inverse, rest * inverse
        weights_ref[m, :, :SEG] = near
        weights_ref[m, :, SEG:] = rest
        near, rest = near.astype(BF16), rest.astype(BF16)
        attn_ref[m] = (dot(near, kvcat[m, :SEG, DH:], (1, 0)) + dot(rest, kvcat[m, SEG:, DH:], (1, 0))).astype(BF16)

    scores = score(0)
    for m in range(A):
        later = score(m + 1) if m + 1 < A else None
        mix(m, *scores)
        scores = later


def backward_body(A, B, score_scale, attn_ref, kvcat, weights_ref, *refs):
    piece_refs, (dq_ref, own_ref, cache_ref, carry_ref) = refs[:A], refs[A:]
    SEG = piece_refs[0].shape[0]
    a = lax.axis_index("seg") % A
    for m in range(A):
        seg_a = a ^ m
        prev_a = jnp.where(seg_a == 0, A - 1, seg_a - 1)
        q, da = piece_refs[m][:, :DH], piece_refs[m][:, DH : 2 * DH]
        row_delta = jnp.sum(da.astype(F32) * attn_ref[m].astype(F32), -1, keepdims=True)
        weights = weights_ref[m]
        rounded = weights.astype(BF16)
        slopes = (weights.astype(F32) * (dot(da, kvcat[m, :, DH:], (1, 1)) - row_delta)).astype(BF16)
        dq_ref[m] = (score_scale * dot(slopes, kvcat[m, :, :DH], (1, 0))).astype(BF16)
        dk = score_scale * dot(slopes[:, : 2 * SEG], q, (0, 0))
        dv = dot(rounded[:, : 2 * SEG], da, (0, 0))
        own_ref[m, :, :DH] = dk[:SEG]
        own_ref[m, :, DH:] = dv[:SEG]
        dk, dv = dk[SEG:].astype(BF16), dv[SEG:].astype(BF16)
        cache_ref[prev_a ^ a, :, :DH] = dk
        cache_ref[prev_a ^ a, :, DH:] = dv

        @pl.when(seg_a == 0)
        def _():
            carry_ref[:, :DH] = dk
            carry_ref[:, DH:] = dv


def project_body(A, B, H, *refs):
    attns, gs, weight_ref, refs = straight(refs[:A]), refs[A : A + 2], refs[A + 2], refs[A + 3 :]
    keep_ref, pass_ref, send_ref, *proj_refs = refs[:-3]
    own, mixed, cots = refs[-3:]
    seg = lax.axis_index("seg")
    a, b = seg % A, seg // A
    h = lax.axis_index("head")
    SEG = attns[0].shape[1]
    for m in range(A):
        head = lanes(a ^ m, DH)
        own[:, head] = attns[m][m]
        for i in range(A):
            mixed[(m ^ i) * SEG : (m ^ i) * SEG + SEG, head] = attns[m][i]
    width = keep_ref.shape[1]
    keep_ref[...] = dot(own[...], weight_ref[:, lanes(h, width)], (1, 0))
    pass_ref[...] = dot(own[...], weight_ref[:, lanes(h ^ 2, width)], (1, 0))
    for k in (1, 3):
        at = k // 2 * width
        send_ref[:, at : at + width] = dot(own[...], weight_ref[:, lanes(h ^ k, width)], (1, 0)).astype(BF16)
    piece = gs[0].shape[3]
    for k in range(H):
        for m in range(A):
            cots[m * SEG : (m + 1) * SEG, lanes(h ^ k, piece)] = gs[k % 2][k // 2, m]
    if B == 2:
        rows = piece * H // 2
        proj_refs[0][...] = dot(cots[:, lanes(b, rows)], mixed[...], (0, 0))
        proj_refs[1][...] = dot(cots[:, lanes(1 - b, rows)], mixed[...], (0, 0)).astype(BF16)
    else:
        proj_refs[0][...] = dot(cots[...], mixed[...], (0, 0))


def merge_body(A, dq_ref, own_ref, cache_ref, carry_ref, *outs):
    a = lax.axis_index("seg") % A
    for m in range(A):
        outs[m][:, :DH] = dq_ref[m]
        late = jnp.where(a ^ m == A - 1, carry_ref[...], cache_ref[m])
        outs[m][:, DH:] = (own_ref[m] + late.astype(F32)).astype(BF16)


def token_body(*refs):
    refs[-1][...] = jnp.zeros_like(refs[-1])


def place_body(A, B, *refs):
    pieces, terms, projs, outs = straight(refs[:A], LAST), refs[A : A + 3], refs[A + 3 : -6], refs[-5:]
    a = lax.axis_index("seg") % A
    for m in range(A):
        for i in range(3):
            outs[1 + i][:, lanes(a ^ m, DH)] = pieces[m][:, i * DH : (i + 1) * DH]
    outs[0][...] = sum(term[...].astype(F32) for term in terms).astype(BF16)
    outs[4][...] = sum(term[...].astype(F32) for term in projs)


def per_device(queries, keys, values, out_grad, out_weight, retr_owner, retr_block):
    n, H = lax.axis_size("seg"), lax.axis_size("head")
    SEG, width = queries.shape
    A = width // DH
    B = n // A
    R = retr_owner.shape[1]
    D = out_weight.shape[1]
    score_scale = 1.0 / math.sqrt(DH)

    def over_a(x, m):
        return lax.ppermute(x, "seg", [(i, i // A * A + (i % A ^ m)) for i in range(n)])

    def over_b(x):
        return lax.ppermute(x, "seg", [(i, (i + A) % n) for i in range(n)])

    def back_b(x):
        return lax.ppermute(x, "seg", [(i, i - A) for i in range(A, n)])

    def over_head(x, k):
        return lax.ppermute(x, "head", [(i, i ^ k) for i in range(H)])

    def exchange(pieces):
        moved = {m: over_a(pieces[m], m) for m in reversed(range(1, A))}
        return [pieces[0]] + [moved[m] for m in range(1, A)]


    cut = functools.partial(cut_body, A, B)
    kvs = call(cut, [shape((SEG, 2 * DH), BF16)] * A, [keys, values])
    out_grad, kvs[0] = lax.optimization_barrier((out_grad, kvs[0]))
    far_grad = over_head(out_grad, 2)
    kvs = exchange(kvs)
    staged = call(stage_body, [shape(x.shape, BF16) for x in (out_weight, queries, out_grad)], [out_weight, queries, out_grad])
    early = [over_b(kvs[0])] if B == 2 else []
    kv = call(
        functools.partial(pack_body, A),
        [shape((A - 1, SEG, 2 * DH), BF16)],
        [*turned(kvs)[:-1], *early, staged[0]],
        specs=[VMEM] * (A - 1) + [ANY] * (1 + len(early)),
        flops=40 * 10**8,
    )[0]
    out_weight, queries, near_grad = staged
    both = call(join_body, [shape((2, SEG, width), BF16)], [near_grad, far_grad])[0]
    grads = [both, over_head(both, 1)]
    if B == 2:
        kv = [*early, over_b(kv)]
    else:
        groups = [[j * A + i for j in range(B)] for i in range(A)]
        kv = lax.all_gather(jnp.concatenate([kvs[0][None], kv]), "seg", axis_index_groups=groups)
        kv = [kv.reshape(B * A * (SEG // BLOCK), BLOCK, 2 * DH)]
    sloped = call(
        functools.partial(slope_body, A, B, H),
        [shape((SEG, 2 * DH + width // H), BF16)] * A,
        [*grads, out_weight, queries],
        scratch=[pltpu.VMEM((SEG, D), BF16), pltpu.VMEM((SEG, width), BF16)],
        flops=1,
    )
    pieces = exchange(sloped)
    count = 2 * SEG + R * BLOCK
    cot = call(collect_body, [shape((A, SEG, width // H), BF16)], pieces)[0]
    far_cot = over_head(cot, 2)
    limit = 20 if B == 2 else 60
    attn, kvcat, weights = call(
        functools.partial(forward_body, A, B, R, score_scale),
        [shape((A, SEG, DH), BF16), shape((A, count, 2 * DH), BF16), shape((A, SEG, count), F32)],
        [retr_owner, retr_block, *turned(pieces, LAST), *kvs, *kv],
        specs=[SMEM] * 2 + [VMEM] * (2 * A + len(kv)),
        scratch=[pltpu.VMEM((2 * A * (SEG // BLOCK), BLOCK, 2 * DH), BF16)],
        limit=limit,
        flops=10**11,
    )
    dq, own, cache, carry = call(
        functools.partial(backward_body, A, B, score_scale),
        [
            shape((A, SEG, DH), BF16),
            shape((A, SEG, 2 * DH), F32),
            shape((A, SEG, 2 * DH), BF16),
            shape((SEG, 2 * DH), BF16),
        ],
        [attn, kvcat, weights, *pieces],
        limit=limit,
        flops=10**11,
    )
    attns = exchange([attn] * A)
    carried = back_b(carry)
    cots = call(join_body, [shape((2, *cot.shape), BF16)], [cot, far_cot])[0]
    gs = [cots, over_head(cots, 1)]
    merged = call(
        functools.partial(merge_body, A),
        [shape((SEG, 3 * DH), BF16)] * A,
        [dq, own, cache, carried],
        flops=10 * 10**9,
    )
    partials = [shape((SEG, D // H), F32)] * 2 + [shape((SEG, D // 2), BF16)]
    rows = D // A
    if B == 2:
        projs = [shape((rows // 2, width), F32), shape((rows // 2, width), BF16)]
    else:
        projs = [shape((rows, width), F32)]
    keep, passed, send, *proj = call(
        functools.partial(project_body, A, B, H),
        partials + projs,
        [*turned(attns), *gs, out_weight],
        specs=[VMEM] * (A + 3),
        scratch=[
            pltpu.VMEM((SEG, width), BF16),
            pltpu.VMEM((A * SEG, width), BF16),
            pltpu.VMEM((A * SEG, rows), BF16),
        ],
    )
    moved = exchange(merged)
    block = D // H
    received = over_head(send, 1)
    passed = (passed + received[:, block:].astype(F32)).astype(BF16)
    if B == 2:
        proj = [proj[0], over_b(proj[1])]
    else:
        proj = [lax.psum_scatter(proj[0], "seg", scatter_dimension=0, axis_index_groups=groups, tiled=True)]
    token = call(token_body, [shape((8, 128), F32)], [*moved[1:], *proj[1:]], specs=[ANY] * (A - 2 + len(proj)), flops=10**11)
    return tuple(
        call(
            functools.partial(place_body, A, B),
            [shape((SEG, width), BF16)] * 4 + [shape(proj[0].shape, F32)],
            [*turned(moved, LAST), keep, received[:, :block], over_head(passed, 2), *proj, *token],
            specs=[VMEM] * (A + 3 + len(proj)) + [ANY],
        )
    )


def solution(mesh):
    both = P("seg", "head")
    return jax.shard_map(
        per_device,
        mesh=mesh,
        in_specs=(both, both, both, both, P("head", None), P(), P()),
        out_specs=(both,) * 5,
        check_vma=False,
    )
```

```python
import functools
import math

import jax
import jax.numpy as jnp
from jax import lax
from jax.experimental import pallas as pl
from jax.experimental.pallas import tpu as pltpu
from jax.sharding import PartitionSpec as P

DH = 128
BLOCK = 128
F32 = jnp.float32
BF16 = jnp.bfloat16
HIDDEN = -1e30
TURN = (2, 3, 1, 0)
LAST = (3, 2, 1, 0)
VMEM = pl.BlockSpec(memory_space=pltpu.VMEM)
ANY = pl.BlockSpec(memory_space=pl.ANY)
HBM = pl.BlockSpec(memory_space=pltpu.HBM)
SMEM = pl.BlockSpec(memory_space=pltpu.SMEM)


def dot(left, right, dims):
    return lax.dot_general(left, right, ((dims[:1], dims[1:]), ((), ())), preferred_element_type=F32)


def lanes(block, width):
    return pl.ds(pl.multiple_of(block * width, width), width)


def turned(pieces, turn=TURN):
    return [pieces[m] for m in turn]


def straight(refs, turn=TURN):
    return [refs[turn.index(m)] for m in range(len(turn))]


def call(body, outs, operands, specs=None, scratch=(), limit=20, flops=1):
    return list(pl.pallas_call(
        body,
        out_shape=outs,
        in_specs=specs or [VMEM] * len(operands),
        out_specs=[VMEM] * len(outs),
        scratch_shapes=list(scratch),
        compiler_params=pltpu.CompilerParams(vmem_limit_bytes=limit * 2**20),
        cost_estimate=pl.CostEstimate(flops=flops, bytes_accessed=1, transcendentals=0),
    )(*operands))


def shape(dims, dtype):
    return jax.ShapeDtypeStruct(dims, dtype)


def cut_body(A, B, k_ref, v_ref, *outs):
    a = lax.axis_index("seg") % A
    for m in range(A):
        head = lanes(a ^ m, DH)
        outs[m][:, :DH] = k_ref[:, head]
        outs[m][:, DH:] = v_ref[:, head]


def cot_piece(full, A, B, H, other, h):
    total = full.shape[1]
    part, own = total // (A * H), total // (A * B)
    if own % part == 0:
        split = own // part
        return full[:, lanes(((h // split) * A + other) * split + h % split, part)]
    row = lax.broadcasted_iota(jnp.int32, (part * A, part), 0)
    col = lax.broadcasted_iota(jnp.int32, (part * A, part), 1)
    pick = (row == (col // own * A + other) * own + col % own).astype(BF16)
    return dot(full[:, lanes(h, part * A)], pick, (1, 0)).astype(BF16)


def slope_body(A, B, H, *refs):
    grads, weight_ref, q_ref, refs = refs[:2], refs[2], refs[3], refs[4:]
    outs, full, mixed = refs[:A], refs[-2], refs[-1]
    a = lax.axis_index("seg") % A
    h = lax.axis_index("head")
    width = grads[0].shape[2]
    for k in range(H):
        full[:, lanes(h ^ k, width)] = grads[k % 2][k // 2]
    mixed[...] = dot(full[...], weight_ref[...], (1, 1)).astype(BF16)
    for m in range(A):
        head = lanes(a ^ m, DH)
        outs[m][:, :DH] = q_ref[:, head]
        outs[m][:, DH : 2 * DH] = mixed[:, head]
        outs[m][:, 2 * DH :] = cot_piece(full, A, B, H, a ^ m, h)


def pack_body(A, *refs):
    for m in range(1, A):
        refs[-1][m - 1] = refs[TURN.index(m)][...]


def collect_body(*refs):
    for m, ref in enumerate(refs[:-1]):
        refs[-1][m] = ref[:, 2 * DH :]


def join_body(*refs):
    for i, ref in enumerate(refs[:-1]):
        refs[-1][i] = ref[...]


def stage_body(*refs):
    half = len(refs) // 2
    for source, target in zip(refs[:half], refs[half:]):
        target[...] = source[...]


def forward_body(A, B, R, score_scale, owner_ref, block_ref, *refs):
    pair = B == 2
    piece_refs, own_refs, others, refs = straight(refs[:A], LAST), refs[A : 2 * A], refs[2 * A : -4], refs[-4:]
    attn_ref, kvcat, weights_ref, kv = refs
    SEG = piece_refs[0].shape[0]
    parts = SEG // BLOCK
    count = 2 * SEG + R * BLOCK
    seg = lax.axis_index("seg")
    a, b = seg % A, seg // A
    if pair:
        for m in range(A):
            for part in range(parts):
                rows = slice(part * BLOCK, (part + 1) * BLOCK)
                kv[m * parts + part] = own_refs[m][rows, :]
                kv[(A + m) * parts + part] = others[1][m - 1, rows, :] if m else others[0][rows, :]
    else:
        kv = others[0]

    def place(other_a, other_b):
        slot = (other_b ^ b) * A + (other_a ^ a) if pair else other_b * A + (other_a ^ a)
        return slot * parts

    row = lax.broadcasted_iota(jnp.int32, (SEG, SEG), 0)
    col = lax.broadcasted_iota(jnp.int32, (SEG, SEG), 1)
    scale = score_scale * math.log2(math.e)
    far = count - SEG
    column = lax.broadcasted_iota(jnp.int32, (1, far), 1)

    def score(m):
        seg_a = a ^ m
        s = b * A + seg_a
        prev_a = jnp.where(seg_a == 0, A - 1, seg_a - 1)
        prev_b = jnp.where(seg_a == 0, (b + B - 1) % B, b)
        hidden = (column < SEG) & (s == 0)
        for part in range(parts):
            at = part * BLOCK
            kvcat[m, at : at + BLOCK] = kv[place(seg_a, b) + part]
            kvcat[m, SEG + at : SEG + at + BLOCK] = kv[place(prev_a, prev_b) + part]
        for j in range(R):
            at = SEG + j * BLOCK
            owner, block = owner_ref[s, j], block_ref[s, j]
            kvcat[m, SEG + at : SEG + at + BLOCK] = kv[place(owner % A, owner // A) + jnp.maximum(block, 0)]
            hidden |= (column >= at) & (column < at + BLOCK) & (block < 0)
        q = piece_refs[m][:, :DH]
        near = jnp.where(row >= col, dot(q, kvcat[m, :SEG, :DH], (1, 1)) * scale, HIDDEN)
        return near, dot(q, kvcat[m, SEG:, :DH], (1, 1)) * scale + jnp.where(hidden, HIDDEN, 0.0)

    def mix(m, near, rest):
        top = jnp.maximum(jnp.max(near, -1, keepdims=True), jnp.max(rest, -1, keepdims=True))
        near, rest = jnp.exp2(near - top), jnp.exp2(rest - top)
        inverse = 1.0 / (jnp.sum(near, -1, keepdims=True) + jnp.sum(rest, -1, keepdims=True))
        near, rest = near * inverse, rest * inverse
        weights_ref[m, :, :SEG] = near
        weights_ref[m, :, SEG:] = rest
        near, rest = near.astype(BF16), rest.astype(BF16)
        attn_ref[m] = (dot(near, kvcat[m, :SEG, DH:], (1, 0)) + dot(rest, kvcat[m, SEG:, DH:], (1, 0))).astype(BF16)

    scores = score(0)
    for m in range(A):
        later = score(m + 1) if m + 1 < A else None
        mix(m, *scores)
        scores = later


def backward_body(A, B, score_scale, attn_ref, kvcat, weights_ref, *refs):
    piece_refs, (dq_ref, own_ref, cache_ref, carry_ref) = refs[:A], refs[A:]
    SEG = piece_refs[0].shape[0]
    a = lax.axis_index("seg") % A
    raw = [dot(piece_refs[0][:, DH : 2 * DH], kvcat[0, :, DH:], (1, 1))]
    for m in range(A):
        seg_a = a ^ m
        if m + 1 < A:
            raw.append(dot(piece_refs[m + 1][:, DH : 2 * DH], kvcat[m + 1, :, DH:], (1, 1)))
        prev_a = jnp.where(seg_a == 0, A - 1, seg_a - 1)
        q, da = piece_refs[m][:, :DH], piece_refs[m][:, DH : 2 * DH]
        row_delta = jnp.sum(da.astype(F32) * attn_ref[m].astype(F32), -1, keepdims=True)
        weights = weights_ref[m]
        rounded = weights.astype(BF16)
        slopes = (weights.astype(F32) * (raw[m] - row_delta)).astype(BF16)
        dq_ref[m] = (score_scale * dot(slopes, kvcat[m, :, :DH], (1, 0))).astype(BF16)
        dk = score_scale * dot(slopes[:, : 2 * SEG], q, (0, 0))
        dv = dot(rounded[:, : 2 * SEG], da, (0, 0))
        own_ref[m, :, :DH] = dk[:SEG]
        own_ref[m, :, DH:] = dv[:SEG]
        dk, dv = dk[SEG:].astype(BF16), dv[SEG:].astype(BF16)
        cache_ref[prev_a ^ a, :, :DH] = dk
        cache_ref[prev_a ^ a, :, DH:] = dv

        @pl.when(seg_a == 0)
        def _():
            carry_ref[:, :DH] = dk
            carry_ref[:, DH:] = dv


def project_body(A, B, H, *refs):
    attns, gs, weight_ref, refs = straight(refs[:A]), refs[A : A + 2], refs[A + 2], refs[A + 3 :]
    keep_ref, pass_ref, send_ref, *proj_refs = refs[:-3]
    own, mixed, cots = refs[-3:]
    seg = lax.axis_index("seg")
    a, b = seg % A, seg // A
    h = lax.axis_index("head")
    SEG = attns[0].shape[1]
    for m in range(A):
        head = lanes(a ^ m, DH)
        own[:, head] = attns[m][m]
        for i in range(A):
            mixed[(m ^ i) * SEG : (m ^ i) * SEG + SEG, head] = attns[m][i]
    width = keep_ref.shape[1]
    keep_ref[...] = dot(own[...], weight_ref[:, lanes(h, width)], (1, 0))
    pass_ref[...] = dot(own[...], weight_ref[:, lanes(h ^ 2, width)], (1, 0))
    for k in (1, 3):
        at = k // 2 * width
        send_ref[:, at : at + width] = dot(own[...], weight_ref[:, lanes(h ^ k, width)], (1, 0)).astype(BF16)
    piece = gs[0].shape[3]
    for k in range(H):
        for m in range(A):
            cots[m * SEG : (m + 1) * SEG, lanes(h ^ k, piece)] = gs[k % 2][k // 2, m]
    if B == 2:
        rows = piece * H // 2
        proj_refs[0][...] = dot(cots[:, lanes(b, rows)], mixed[...], (0, 0))
        proj_refs[1][...] = dot(cots[:, lanes(1 - b, rows)], mixed[...], (0, 0)).astype(BF16)
    else:
        proj_refs[0][...] = dot(cots[...], mixed[...], (0, 0))


def merge_body(A, dq_ref, own_ref, cache_ref, carry_ref, *outs):
    a = lax.axis_index("seg") % A
    for m in range(A):
        outs[m][:, :DH] = dq_ref[m]
        late = jnp.where(a ^ m == A - 1, carry_ref[...], cache_ref[m])
        outs[m][:, DH:] = (own_ref[m] + late.astype(F32)).astype(BF16)


def token_body(*refs):
    refs[-1][...] = jnp.zeros_like(refs[-1])


def place_body(A, B, *refs):
    pieces, terms, projs, outs = straight(refs[:A], LAST), refs[A : A + 3], refs[A + 3 : -6], refs[-5:]
    a = lax.axis_index("seg") % A
    for m in range(A):
        for i in range(3):
            outs[1 + i][:, lanes(a ^ m, DH)] = pieces[m][:, i * DH : (i + 1) * DH]
    outs[0][...] = sum(term[...].astype(F32) for term in terms).astype(BF16)
    outs[4][...] = sum(term[...].astype(F32) for term in projs)


def per_device(queries, keys, values, out_grad, out_weight, retr_owner, retr_block):
    n, H = lax.axis_size("seg"), lax.axis_size("head")
    SEG, width = queries.shape
    A = width // DH
    B = n // A
    R = retr_owner.shape[1]
    D = out_weight.shape[1]
    score_scale = 1.0 / math.sqrt(DH)

    def over_a(x, m):
        return lax.ppermute(x, "seg", [(i, i // A * A + (i % A ^ m)) for i in range(n)])

    def over_b(x):
        return lax.ppermute(x, "seg", [(i, (i + A) % n) for i in range(n)])

    def back_b(x):
        return lax.ppermute(x, "seg", [(i, i - A) for i in range(A, n)])

    def over_head(x, k):
        return lax.ppermute(x, "head", [(i, i ^ k) for i in range(H)])

    def exchange(pieces):
        moved = {m: over_a(pieces[m], m) for m in reversed(range(1, A))}
        return [pieces[0]] + [moved[m] for m in range(1, A)]


    cut = functools.partial(cut_body, A, B)
    kvs = call(cut, [shape((SEG, 2 * DH), BF16)] * A, [keys, values])
    out_grad, kvs[0] = lax.optimization_barrier((out_grad, kvs[0]))
    far_grad = over_head(out_grad, 2)
    kvs = exchange(kvs)
    staged = call(stage_body, [shape(x.shape, BF16) for x in (out_weight, queries, out_grad)], [out_weight, queries, out_grad])
    early = [over_b(kvs[0])] if B == 2 else []
    kv = call(
        functools.partial(pack_body, A),
        [shape((A - 1, SEG, 2 * DH), BF16)],
        [*turned(kvs)[:-1], *early, staged[0]],
        specs=[VMEM] * (A - 1) + [ANY] * (1 + len(early)),
        flops=40 * 10**8,
    )[0]
    out_weight, queries, near_grad = staged
    both = call(join_body, [shape((2, SEG, width), BF16)], [near_grad, far_grad])[0]
    grads = [both, over_head(both, 1)]
    if B == 2:
        kv = [*early, over_b(kv)]
    else:
        groups = [[j * A + i for j in range(B)] for i in range(A)]
        kv = lax.all_gather(jnp.concatenate([kvs[0][None], kv]), "seg", axis_index_groups=groups)
        kv = [kv.reshape(B * A * (SEG // BLOCK), BLOCK, 2 * DH)]
    sloped = call(
        functools.partial(slope_body, A, B, H),
        [shape((SEG, 2 * DH + width // H), BF16)] * A,
        [*grads, out_weight, queries],
        scratch=[pltpu.VMEM((SEG, D), BF16), pltpu.VMEM((SEG, width), BF16)],
        flops=1,
    )
    pieces = exchange(sloped)
    count = 2 * SEG + R * BLOCK
    cot = call(collect_body, [shape((A, SEG, width // H), BF16)], pieces)[0]
    far_cot = over_head(cot, 2)
    limit = 20 if B == 2 else 60
    attn, kvcat, weights = call(
        functools.partial(forward_body, A, B, R, score_scale),
        [shape((A, SEG, DH), BF16), shape((A, count, 2 * DH), BF16), shape((A, SEG, count), F32)],
        [retr_owner, retr_block, *turned(pieces, LAST), *kvs, *kv],
        specs=[SMEM] * 2 + [VMEM] * (2 * A + len(kv)),
        scratch=[pltpu.VMEM((2 * A * (SEG // BLOCK), BLOCK, 2 * DH), BF16)],
        limit=limit,
        flops=10**11,
    )
    dq, own, cache, carry = call(
        functools.partial(backward_body, A, B, score_scale),
        [
            shape((A, SEG, DH), BF16),
            shape((A, SEG, 2 * DH), F32),
            shape((A, SEG, 2 * DH), BF16),
            shape((SEG, 2 * DH), BF16),
        ],
        [attn, kvcat, weights, *pieces],
        limit=limit,
        flops=10**11,
    )
    attns = exchange([attn] * A)
    carried = back_b(carry)
    cots = call(join_body, [shape((2, *cot.shape), BF16)], [cot, far_cot])[0]
    gs = [cots, over_head(cots, 1)]
    merged = call(
        functools.partial(merge_body, A),
        [shape((SEG, 3 * DH), BF16)] * A,
        [dq, own, cache, carried],
        flops=10 * 10**9,
    )
    partials = [shape((SEG, D // H), F32)] * 2 + [shape((SEG, D // 2), BF16)]
    rows = D // A
    if B == 2:
        projs = [shape((rows // 2, width), F32), shape((rows // 2, width), BF16)]
    else:
        projs = [shape((rows, width), F32)]
    keep, passed, send, *proj = call(
        functools.partial(project_body, A, B, H),
        partials + projs,
        [*turned(attns), *gs, out_weight],
        specs=[VMEM] * (A + 3),
        scratch=[
            pltpu.VMEM((SEG, width), BF16),
            pltpu.VMEM((A * SEG, width), BF16),
            pltpu.VMEM((A * SEG, rows), BF16),
        ],
    )
    moved = exchange(merged)
    block = D // H
    received = over_head(send, 1)
    passed = (passed + received[:, block:].astype(F32)).astype(BF16)
    if B == 2:
        proj = [proj[0], over_b(proj[1])]
    else:
        proj = [lax.psum_scatter(proj[0], "seg", scatter_dimension=0, axis_index_groups=groups, tiled=True)]
    token = call(token_body, [shape((8, 128), F32)], [*moved[1:], *proj[1:]], specs=[ANY] * (A - 2 + len(proj)), flops=10**11)
    return tuple(
        call(
            functools.partial(place_body, A, B),
            [shape((SEG, width), BF16)] * 4 + [shape(proj[0].shape, F32)],
            [*turned(moved, LAST), keep, received[:, :block], over_head(passed, 2), *proj, *token],
            specs=[VMEM] * (A + 3 + len(proj)) + [ANY],
        )
    )


def solution(mesh):
    both = P("seg", "head")
    return jax.shard_map(
        per_device,
        mesh=mesh,
        in_specs=(both, both, both, both, P("head", None), P(), P()),
        out_specs=(both,) * 5,
        check_vma=False,
    )
```
